32 devices in a mesh: rows: 8 (over z, y), px: 4 (over x, core).
Axes of the slice: x: 2, y: 2, z: 4, core: 2. Of those that a mesh axis runs over, the one named last changes fastest.
Arguments:
- queries: float32 [8, 65536], P(None, 'rows'), may hold values from -6 to 6
- pixel_mean: float32 [65536], P('rows'), may hold values from -3 to 3
- eigenbasis: bfloat16 [65536, 4096], P('rows', 'px'), may hold values from -0.0234375 to 0.0234375
- eigenvalues: float32 [4096], P('px'), may hold values from 0.05 to 5
- level_ids: int32 [5, 8], replicated, may hold values from 0 to 63
- slab: bfloat16 [4096, 65536], P('rows', 'px'), may hold values from -16 to 16
- slab_classes: int32 [4096], P('rows'), may hold values from 0 to 9
- target_categories: int32 [8], replicated, may hold values from 0 to 9
Outputs:
- denoised: float32 [8, 65536], P(None, 'px')
The draws below stay inside these ranges and needn't reach their ends.
All inputs are finite; a program needn't handle non-finite values.
Results may differ from the reference program's by a relative error of at most 0.0005.
Values sent between devices are 32-bit elements; how exact they have to be, the bound alone decides.
No kernel may reach another device: no remote copies, remote signals or barrier semaphores. Data moves between devices by JAX's collectives and lax.ppermute only.
A program may use at most 128 MiB of HBM per device.

```python
import math
import jax
import jax.numpy as jnp
from jax import lax

IMAGE_POINTS = 65536
COMP = 4096
QUERIES = 8
ROWS_DEV = 512
LEVELS = 64
CLASSES = 10
GSTEPS = 2
ESTEPS = 2
SLAB = 4096


def draw_slab(key, part):
    key_columns = jax.random.fold_in(key, 11)
    key_entries = jax.random.fold_in(key, 13)
    offset = jnp.sqrt(jnp.float32(350.0) / jnp.sqrt(jnp.float32(IMAGE_POINTS)))
    level = jax.random.uniform(key_columns, (IMAGE_POINTS,), jnp.float32, 0.0, 1.0)
    column_scale = 0.216 * jnp.power(10.0, level)
    spread = jax.random.truncated_normal(key_entries, -4.0, 4.0, (SLAB, IMAGE_POINTS), jnp.float32)
    values = column_scale[None, :] * spread + offset
    return jnp.clip(values, -16.0, 16.0).astype(jnp.bfloat16)


def set_ends(entries, rng, least, largest):
    longest = entries.shape.index(max(entries.shape))
    spots = []
    for shift in (0, 1):
        where = [jax.random.randint(jax.random.fold_in(rng, axis), (), 0, length) for axis, length in enumerate(entries.shape)]
        where[longest] = (where[longest] + shift) % entries.shape[longest]
        spots.append(tuple(where))
    return entries.at[spots[0]].set(least).at[spots[1]].set(largest)


def steps_of(key, extent, pieces, smallest, high):
    def one(position, shards_of):
        draws = jax.random.uniform(jax.random.fold_in(jax.random.fold_in(key, 6), position), (shards_of,), jnp.float32, smallest / len(pieces), high / len(pieces))
        return jnp.repeat(jnp.exp(draws), extent[position] // shards_of).reshape((-1,) + (1,) * (len(extent) - position - 1))

    gain = one(*pieces[0])
    for cut in pieces[1:]:
        gain = gain * one(*cut)
    return gain


def centred(own_key, dims, deviation, most, split=(), held_as=jnp.bfloat16):
    factor_of = steps_of(own_key, dims, split, -0.22, 0.18) if split else 1.0
    values = jax.random.normal(own_key, dims, jnp.float32) * deviation * factor_of
    return jnp.minimum(jnp.maximum(values, -most), most).astype(held_as)


def setup_inputs(seed: int = 0) -> dict:
    key_list = jax.random.split(jax.random.key(seed), 9)
    return {
        "queries": centred(key_list[0], (QUERIES, IMAGE_POINTS), 1.0, 6.0, ((1, 8),), jnp.float32),
        "pixel_mean": centred(key_list[1], (IMAGE_POINTS,), 0.5, 3.0, ((0, 8),), jnp.float32),
        "eigenbasis": centred(key_list[2], (IMAGE_POINTS, COMP), IMAGE_POINTS ** -0.5, 0.0234375, ((0, 8), (1, 4))),
        "eigenvalues": jnp.clip(jnp.exp(math.log(5.0) - 4.6051702 * jax.random.uniform(key_list[3], (COMP,), jnp.float32) ** steps_of(key_list[3], (COMP,), ((0, 4),), -0.2, 0.2)), 0.05, 5.0),
        "level_ids": set_ends(jax.random.randint(key_list[4], (GSTEPS + ESTEPS + 1, QUERIES), 0, LEVELS), jax.random.fold_in(key_list[4], 1), 0, LEVELS - 1).astype(jnp.int32),
        "slab": draw_slab(jax.random.fold_in(key_list[8], 71), 0),
        "slab_classes": set_ends(jax.random.randint(key_list[6], (SLAB,), 0, CLASSES), jax.random.fold_in(key_list[6], 1), 0, CLASSES - 1).astype(jnp.int32),
        "target_categories": set_ends(jax.random.randint(key_list[7], (QUERIES,), 0, CLASSES), jax.random.fold_in(key_list[7], 1), 0, CLASSES - 1).astype(jnp.int32),
    }


steering_strength = 1.5
rms_epsilon = 1e-06

def noise_levels(level_ids):
    fraction = level_ids.astype(jnp.float32) / (LEVELS - 1)
    return 0.6 * jnp.exp2(fraction)

def reference(queries, pixel_mean, eigenbasis, eigenvalues, level_ids, slab, slab_classes, target_categories):
    noise_sample = noise_levels(level_ids)
    latent = queries
    for step in range(GSTEPS):
        active_sigma_index = noise_sample[step]
        following_level = noise_sample[step + 1]
        centered = (latent - pixel_mean[None, :]).astype(jnp.bfloat16)
        coefficients = jnp.dot(centered, eigenbasis, preferred_element_type=jnp.float32)
        shrink = eigenvalues[None, :] / (eigenvalues[None, :] + (active_sigma_index * active_sigma_index)[:, None])
        shrunk = (coefficients * shrink).astype(jnp.bfloat16)
        backward = jnp.dot(shrunk, eigenbasis.T, preferred_element_type=jnp.float32)
        cleaned = pixel_mean[None, :] + backward
        latent = cleaned + (following_level / active_sigma_index)[:, None] * (latent - cleaned)
    training_tiles = slab.reshape(-1, ROWS_DEV, IMAGE_POINTS)
    tile_categories = slab_classes.reshape(-1, ROWS_DEV)
    category_reward = jnp.where(tile_categories[:, None, :] == target_categories[None, :, None], steering_strength, 0.0).astype(jnp.float32)
    magnitude_normalizer = jnp.ones((QUERIES,), jnp.float32)
    for step in range(ESTEPS):
        level_row = GSTEPS + step
        active_sigma_index = noise_sample[level_row]
        following_level = noise_sample[level_row + 1]
        sharpness_factor = 1.0 / (2.0 * active_sigma_index * active_sigma_index * math.sqrt(IMAGE_POINTS))
        operand = latent.astype(jnp.bfloat16)

        def lone_tile(paired_blocks):
            rows_in_block, entry_rewards = paired_blocks
            pairwise_similarity = jnp.dot(operand, rows_in_block.T, preferred_element_type=jnp.float32)
            training_vector_energies = lax.optimization_barrier(jnp.sum(jnp.square(rows_in_block.astype(jnp.float32)), axis=1))
            unnormalized_affinity = sharpness_factor[:, None] * (2.0 * pairwise_similarity / magnitude_normalizer[:, None] - training_vector_energies[None, :]) + entry_rewards
            block_peak = lax.optimization_barrier(jnp.max(unnormalized_affinity, axis=1))
            weights = jnp.exp(unnormalized_affinity - block_peak[:, None]).astype(jnp.bfloat16)
            weight_mass = lax.optimization_barrier(jnp.sum(weights.astype(jnp.float32), axis=1))
            weighted = jnp.dot(weights, rows_in_block, preferred_element_type=jnp.float32)
            return (block_peak, weight_mass, weighted)
        cumulative_maxima, normalized_probabilities, cumulative_denominators = lax.map(lone_tile, (training_tiles, category_reward))
        overall = lax.optimization_barrier(jnp.max(cumulative_maxima, axis=0))
        rescale = jnp.exp(cumulative_maxima - overall[None, :])
        denominator = lax.optimization_barrier(jnp.sum(rescale * normalized_probabilities, axis=0))
        average = lax.optimization_barrier(jnp.sum(rescale[:, :, None] * cumulative_denominators, axis=0)) / denominator[:, None]
        current_latent = latent / magnitude_normalizer[:, None]
        updated_latent = average + (following_level / active_sigma_index)[:, None] * (current_latent - average)
        magnitude_normalizer = jnp.sqrt(lax.optimization_barrier(jnp.mean(updated_latent * updated_latent, axis=1)) + rms_epsilon)
        latent = updated_latent
    return latent / magnitude_normalizer[:, None]
```

```python
import functools
import math

import jax
import jax.numpy as jnp
from jax import lax
from jax.experimental import pallas as pl
from jax.experimental.pallas import tpu as pltpu
from jax.sharding import PartitionSpec as P

IMAGE_POINTS = 65536
LEVELS = 64
STEERING = 1.5
RMS_EPSILON = 1e-06
MIB = 1024 * 1024
NT = (((1,), (1,)), ((), ()))
CHUNKS = 8
PAD = 128

f32 = jnp.float32
bf16 = jnp.bfloat16


def vmem():
    return pl.BlockSpec(memory_space=pltpu.VMEM)


def anywhere():
    return pl.BlockSpec(memory_space=pl.ANY)


def in_vmem(x):
    return pltpu.with_memory_space_constraint(x, pltpu.VMEM)


def shape(dims, dtype=f32):
    return jax.ShapeDtypeStruct(dims, dtype)


def call(kernel, out_shape, args, in_specs=None, scratch=(), flops=0, name=None):
    many = isinstance(out_shape, (list, tuple))
    return pl.pallas_call(
        kernel,
        in_specs=in_specs or [vmem()] * len(args),
        out_specs=[vmem()] * len(out_shape) if many else vmem(),
        out_shape=out_shape,
        scratch_shapes=list(scratch),
        compiler_params=pltpu.CompilerParams(vmem_limit_bytes=10 * MIB),
        cost_estimate=pl.CostEstimate(
            flops=flops, bytes_accessed=16 * MIB if flops else MIB, transcendentals=0
        ),
        name=name,
    )(*args)


def rows_at(start, count, unit):
    return pl.ds(pl.multiple_of(start, unit), count)


def load_project_kernel(q_hbm, mean_hbm, e_hbm, copies, offset, e_vmem, q, mean, sems):
    pixels = e_hbm.shape[0]
    chunk = pixels // CHUNKS

    def moves(c):
        at = rows_at(c * chunk, chunk, chunk)
        return (
            pltpu.make_async_copy(q_hbm.at[:, at], q.at[:, at], sems.at[c, 0]),
            pltpu.make_async_copy(mean_hbm.at[:, at], mean.at[:, at], sems.at[c, 1]),
            pltpu.make_async_copy(e_hbm.at[at], e_vmem.at[at], sems.at[c, 2]),
        )

    @pl.loop(0, CHUNKS)
    def _(c):
        for move in moves(c):
            move.start()

    def step(c, total):
        for move in moves(c):
            move.wait()
        at = rows_at(c * chunk, chunk, chunk)
        off = q[:, at] - mean[:, at]
        offset[:, at] = off
        return total + jnp.dot(off.astype(bf16), e_vmem[at, :], preferred_element_type=f32)

    total = lax.fori_loop(0, CHUNKS, step, jnp.zeros((8, e_hbm.shape[1]), f32))
    for k in range(copies.shape[0]):
        copies[k] = total


def load_project(queries, mean, basis, row_count):
    pixels, comps = basis.shape
    basis = pltpu.with_memory_space_constraint(basis, pltpu.HBM)
    return call(
        load_project_kernel,
        [
            shape((row_count, 8, comps)),
            shape((8, pixels)),
            pltpu.VMEM((pixels, comps), bf16),
        ],
        (queries, mean, basis),
        in_specs=[anywhere()] * 3,
        scratch=[
            pltpu.VMEM((8, pixels), f32),
            pltpu.VMEM((1, pixels), f32),
            pltpu.SemaphoreType.DMA((CHUNKS, 3)),
        ],
        flops=16 * pixels * comps,
        name="load_project",
    )


def back_kernel(step, flip, parts, eigenvalues, sigma, e_vmem, image):
    half = image.shape[1]
    core = lax.rem(lax.axis_index("px"), 2)
    which = 1 - core if flip else core
    now = sigma[:, step : step + 1]
    coeff = jnp.sum(parts[...], axis=0)
    ev = eigenvalues[...]
    shrunk = (coeff * (ev / (ev + now * now))).astype(bf16)
    tile = min(1024, half)

    @pl.loop(0, half // tile)
    def _(i):
        at = rows_at(which * half + i * tile, tile, tile)
        image[:, rows_at(i * tile, tile, tile)] = lax.dot_general(
            shrunk, e_vmem[at, :], NT, preferred_element_type=f32
        )


def back(step, flip, parts, eigenvalues, sigma, e_vmem):
    pixels, comps = e_vmem.shape
    return call(
        functools.partial(back_kernel, step, flip),
        shape((8, pixels // 2)),
        (parts, eigenvalues, sigma, in_vmem(e_vmem)),
        flops=8 * pixels * comps,
        name=f"back_{step}_{int(flip)}",
    )


def project_half_kernel(flip, off, e_vmem, out):
    half = off.shape[1]
    core = lax.rem(lax.axis_index("px"), 2)
    which = 1 - core if flip else core
    tile = min(1024, half)

    def step(i, total):
        at = rows_at(which * half + i * tile, tile, tile)
        part = off[:, rows_at(i * tile, tile, tile)].astype(bf16)
        return total + jnp.dot(part, e_vmem[at, :], preferred_element_type=f32)

    out[...] = lax.fori_loop(0, half // tile, step, jnp.zeros(out.shape, f32))


def project_rest_kernel(off, own, e_vmem, copies):
    half = off.shape[1]
    which = 1 - lax.rem(lax.axis_index("px"), 2)
    tile = min(1024, half)

    def step(i, total):
        at = rows_at(which * half + i * tile, tile, tile)
        part = off[:, rows_at(i * tile, tile, tile)].astype(bf16)
        return total + jnp.dot(part, e_vmem[at, :], preferred_element_type=f32)

    total = lax.fori_loop(0, half // tile, step, own[...])
    for k in range(copies.shape[0]):
        copies[k] = total


def first_update_kernel(mine, theirs, offset, sigma, out):
    half = mine.shape[1]
    core = lax.rem(lax.axis_index("px"), 2)
    ratio = sigma[:, 1:2] / sigma[:, 0:1]
    image = mine[...] + theirs[...]
    out[...] = image + ratio * (offset[:, rows_at(core * half, half, half)] - image)


def second_update_kernel(mine, theirs, offset, mean, sigma, out):
    half = mine.shape[1]
    span = half // 2
    place = lax.axis_index("px")
    core = lax.rem(place, 2)
    x = lax.div(place, 2)
    ratio = sigma[:, 2:3] / sigma[:, 1:2]
    image = mine[...] + theirs[...]
    first = jnp.where(x == 0, 1.0, 0.0).astype(f32)
    mean_half = mean[:, rows_at(core * half, half, half)]
    sent = (1.0 - ratio) * image + first * (ratio * offset[...] + mean_half)
    for k in range(2):
        out[lax.rem(k + x, 2)] = sent[:, k * span : (k + 1) * span]


def norms_kernel(slab, out):
    rows, pixels = slab.shape
    tile = 1024

    def step(i, total):
        part = slab[:, rows_at(i * tile, tile, tile)].astype(f32)
        square = part * part
        for k in range(tile // 128):
            total = total + square[:, k * 128 : (k + 1) * 128]
        return total

    total = lax.fori_loop(0, pixels // tile, step, jnp.zeros((rows, 128), f32))
    out[...] = jnp.sum(total, axis=1)[None, :]


def dots_kernel(first, pieces, extra, slab, out):
    count, _, width = pieces.shape
    span = slab.shape[1] // count

    def step(k, total):
        part = pieces[k, :, :span].astype(bf16)
        at = rows_at(k * span, span, span)
        return total + lax.dot_general(part, slab[:, at], NT, preferred_element_type=f32)

    out[:8] = lax.fori_loop(0, count, step, jnp.zeros((8, slab.shape[0]), f32))
    if first:
        out[8:] = jnp.broadcast_to(extra[...], (8, slab.shape[0]))
    else:
        squares = jnp.sum(pieces[:, :, span:], axis=0)[:, :1]
        out[8:] = jnp.broadcast_to(squares, (8, slab.shape[0]))


def weighted_kernel(step, gathered, norms, classes, targets, sigma, slab, out, *aside):
    count, _, width = out.shape
    span = width - PAD
    both = jnp.sum(gathered[...], axis=0)
    dots = both[:8]
    if step == 0:
        norm = both[8:9]
        aside[0][...] = norm
    else:
        norm = norms[...]
        scale = jnp.sqrt(both[8:, :1] / IMAGE_POINTS + RMS_EPSILON)
        dots = dots / scale
        aside[0][...] = jnp.broadcast_to(scale, aside[0].shape)
    now = sigma[:, 2 + step : 3 + step]
    sharp = 1.0 / (2.0 * now * now * math.sqrt(IMAGE_POINTS))
    bonus = jnp.where(classes[...] == targets[...], STEERING, 0.0).astype(f32)
    scores = sharp * (2.0 * dots - norm) + bonus
    peak = jnp.max(scores, axis=1, keepdims=True)
    weights = jnp.exp(scores - peak).astype(bf16)
    mass = jnp.sum(weights.astype(f32), axis=1, keepdims=True)
    lane = lax.broadcasted_iota(jnp.int32, (8, PAD), 1)
    tail = jnp.where(lane < PAD // 2, peak, mass)

    @pl.loop(0, count)
    def _(k):
        at = rows_at(k * span, span, span)
        out[k, :, :span] = jnp.dot(weights, slab[:, at], preferred_element_type=f32)
        out[k, :, span:] = tail


def combine_kernel(step, parts, state, scale, sigma, copies):
    count, _, width = parts.shape
    span = width - PAD
    peaks = [parts[k, :, span : span + 1] for k in range(count)]
    top = functools.reduce(jnp.maximum, peaks)
    total, mass = jnp.zeros((8, span), f32), jnp.zeros((8, 1), f32)
    for k in range(count):
        factor = jnp.exp(peaks[k] - top)
        total = total + factor * parts[k, :, :span]
        mass = mass + factor * parts[k, :, span + PAD // 2 : span + PAD // 2 + 1]
    average = total / mass
    ratio = sigma[:, 3 + step : 4 + step] / sigma[:, 2 + step : 3 + step]
    current = state[...] if step == 0 else state[...] / scale[:, :1]
    update = average + ratio * (current - average)
    square = jnp.broadcast_to(jnp.sum(update * update, axis=1, keepdims=True), (8, PAD))
    for k in range(count):
        copies[k, :, :span] = update
        copies[k, :, span:] = square


def squares_kernel(pieces, out):
    span = pieces.shape[2] - PAD
    out[...] = jnp.sum(pieces[:, :, span:], axis=0)


def finish_kernel(pieces, squares, out):
    count, _, width = pieces.shape
    span = width - PAD
    total = jnp.sum(squares[...], axis=0)[:, :1]
    scale = jnp.sqrt(total / IMAGE_POINTS + RMS_EPSILON)

    @pl.loop(0, count)
    def _(k):
        out[:, rows_at(k * span, span, span)] = pieces[k, :, :span] / scale


def exchange_px(x, flip):
    size = lax.axis_size("px")
    return lax.ppermute(x, "px", [(i, i ^ flip) for i in range(size)])


def swap_rows(x):
    return lax.all_to_all(x, "rows", 0, 0, tiled=True)


def to_slices(x, turn):
    rows, px = lax.axis_size("rows"), lax.axis_size("px")
    pairs = []
    for r in range(rows):
        for p in range(px):
            upper, core = divmod(p, 2)
            piece = r * px + 2 * core + (upper + turn) % 2
            pairs.append((r * px + p, (piece % rows) * px + piece // rows))
    return lax.ppermute(x, ("rows", "px"), pairs)


def shards(
    queries, pixel_mean, eigenbasis, eigenvalues, level_ids, slab, slab_classes, target_categories
):
    rows = lax.axis_size("rows")
    pixels, comps = eigenbasis.shape
    slab_rows, slab_pixels = slab.shape
    span = slab_pixels // rows
    sigma = 0.6 * jnp.exp2(level_ids.T.astype(f32) / (LEVELS - 1))
    mean = pixel_mean[None, :]
    values = eigenvalues[None, :]
    classes = slab_classes[None, :]
    targets = target_categories[:, None]
    gauss_flops = 8 * pixels * comps
    slab_flops = 16 * slab_rows * slab_pixels

    copies, offset, basis = load_project(queries, mean, eigenbasis, rows)
    parts = swap_rows(copies)
    sent = exchange_px(back(0, True, parts, values, sigma, basis), 1)
    image = back(0, False, parts, values, sigma, basis) + sent
    across = exchange_px(image, 2)
    norms = call(
        norms_kernel,
        shape((1, slab_rows)),
        (in_vmem(slab),),
        flops=2 * slab_rows * slab_pixels,
        name="norms",
    )
    offset = call(
        first_update_kernel,
        shape((8, pixels // 2)),
        (image, across, offset, sigma),
        name="first_update",
    )
    other = exchange_px(offset, 1)
    own = call(
        functools.partial(project_half_kernel, False),
        shape((8, comps)),
        (offset, in_vmem(basis)),
        flops=gauss_flops,
        name="project_own",
    )
    copies = call(
        project_rest_kernel,
        shape((rows, 8, comps)),
        (other, own, in_vmem(basis)),
        flops=gauss_flops,
        name="project_rest",
    )
    parts = swap_rows(copies)
    sent = exchange_px(back(1, True, parts, values, sigma, basis), 1)
    mine = back(1, False, parts, values, sigma, basis)
    outgoing = call(
        second_update_kernel,
        shape((2, 8, span)),
        (mine, sent, offset, mean, sigma),
        name="second_update",
    )
    state = to_slices(outgoing[0], 0) + to_slices(outgoing[1], 1)
    pieces = swap_rows(jnp.broadcast_to(state[None], (rows, 8, span)))
    products = call(
        functools.partial(dots_kernel, True),
        shape((16, slab_rows)),
        (pieces, norms, in_vmem(slab)),
        flops=slab_flops,
        name="dots_0",
    )
    scale = None
    for step in range(2):
        gathered = lax.all_gather(products, "px")
        weighted, aside = call(
            functools.partial(weighted_kernel, step),
            [
                shape((rows, 8, span + PAD)),
                shape((1, slab_rows)) if step == 0 else shape((8, PAD)),
            ],
            (gathered, norms, classes, targets, sigma, in_vmem(slab)),
            flops=slab_flops,
            name=f"weighted_{step}",
        )
        if step == 0:
            norms = aside
        else:
            scale = aside
        parts = swap_rows(weighted)
        copies = call(
            functools.partial(combine_kernel, step),
            shape((rows, 8, span + PAD)),
            (parts, state, sigma if scale is None else scale, sigma),
            name=f"combine_{step}",
        )
        state = copies[0, :, :span]
        pieces = swap_rows(copies)
        if step == 0:
            products = call(
                functools.partial(dots_kernel, False),
                shape((16, slab_rows)),
                (pieces, norms, in_vmem(slab)),
                flops=slab_flops,
                name="dots_1",
            )
    squares = call(squares_kernel, shape((8, PAD)), (pieces,), name="squares")
    squares = lax.all_gather(squares, "px")
    return call(finish_kernel, shape((8, slab_pixels)), (pieces, squares), name="finish")


def solution(mesh):
    in_specs = (
        P(None, "rows"),
        P("rows"),
        P("rows", "px"),
        P("px"),
        P(),
        P("rows", "px"),
        P("rows"),
        P(),
    )
    out_specs = P(None, "px")
    return jax.shard_map(shards, mesh=mesh, in_specs=in_specs, out_specs=out_specs, check_vma=False)
```

```python
import functools
import math

import jax
import jax.numpy as jnp
from jax import lax
from jax.experimental import pallas as pl
from jax.experimental.pallas import tpu as pltpu
from jax.sharding import PartitionSpec as P

IMAGE_POINTS = 65536
LEVELS = 64
STEERING = 1.5
RMS_EPSILON = 1e-06
MIB = 1024 * 1024
NT = (((1,), (1,)), ((), ()))
CHUNKS = 8
PAD = 128

f32 = jnp.float32
bf16 = jnp.bfloat16


def vmem():
    return pl.BlockSpec(memory_space=pltpu.VMEM)


def anywhere():
    return pl.BlockSpec(memory_space=pl.ANY)


def in_vmem(x):
    return pltpu.with_memory_space_constraint(x, pltpu.VMEM)


def shape(dims, dtype=f32):
    return jax.ShapeDtypeStruct(dims, dtype)


def call(kernel, out_shape, args, in_specs=None, scratch=(), flops=0, name=None):
    many = isinstance(out_shape, (list, tuple))
    return pl.pallas_call(
        kernel,
        in_specs=in_specs or [vmem()] * len(args),
        out_specs=[vmem()] * len(out_shape) if many else vmem(),
        out_shape=out_shape,
        scratch_shapes=list(scratch),
        compiler_params=pltpu.CompilerParams(vmem_limit_bytes=10 * MIB),
        cost_estimate=pl.CostEstimate(
            flops=flops, bytes_accessed=16 * MIB if flops else MIB, transcendentals=0
        ),
        name=name,
    )(*args)


def rows_at(start, count, unit):
    return pl.ds(pl.multiple_of(start, unit), count)


def column(row):
    count = row.shape[1]
    down = lax.broadcasted_iota(jnp.int32, (count, count), 0)
    across = lax.broadcasted_iota(jnp.int32, (count, count), 1)
    return jnp.sum(jnp.where(down == across, row, 0.0), axis=1, keepdims=True)


def load_project_kernel(
    q_hbm, mean_hbm, e_hbm, levels, copies, offset, e_vmem, sigma, mean, q, sems
):
    pixels = e_hbm.shape[0]
    chunk = pixels // CHUNKS

    def moves(c):
        at = rows_at(c * chunk, chunk, chunk)
        return (
            pltpu.make_async_copy(q_hbm.at[:, at], q.at[:, at], sems.at[c, 0]),
            pltpu.make_async_copy(mean_hbm.at[:, at], mean.at[:, at], sems.at[c, 1]),
            pltpu.make_async_copy(e_hbm.at[at], e_vmem.at[at], sems.at[c, 2]),
        )

    @pl.loop(0, CHUNKS)
    def _(c):
        for move in moves(c):
            move.start()

    lane = lax.broadcasted_iota(jnp.int32, sigma.shape, 1)
    table = jnp.zeros(sigma.shape, f32)
    for t in range(levels.shape[0]):
        fraction = column(levels[t : t + 1, :].astype(f32)) / (LEVELS - 1)
        table = jnp.where(lane == t, 0.6 * jnp.exp2(fraction), table)
    sigma[...] = table

    def step(c, total):
        for move in moves(c):
            move.wait()
        at = rows_at(c * chunk, chunk, chunk)
        off = q[:, at] - mean[:, at]
        offset[:, at] = off
        return total + jnp.dot(off.astype(bf16), e_vmem[at, :], preferred_element_type=f32)

    total = lax.fori_loop(0, CHUNKS, step, jnp.zeros((8, e_hbm.shape[1]), f32))
    for k in range(copies.shape[0]):
        copies[k] = total


def load_project(queries, mean, basis, levels, row_count):
    pixels, comps = basis.shape
    queries, mean, basis = [
        pltpu.with_memory_space_constraint(x, pltpu.HBM) for x in (queries, mean, basis)
    ]
    return call(
        load_project_kernel,
        [
            shape((row_count, 8, comps)),
            shape((8, pixels)),
            pltpu.VMEM((pixels, comps), bf16),
            shape((8, PAD)),
            shape((1, pixels)),
        ],
        (queries, mean, basis, levels),
        in_specs=[anywhere()] * 3 + [vmem()],
        scratch=[
            pltpu.VMEM((8, pixels), f32),
            pltpu.SemaphoreType.DMA((CHUNKS, 3)),
        ],
        flops=16 * pixels * comps,
        name="load_project",
    )


def back_kernel(step, flip, parts, eigenvalues, sigma, e_vmem, image):
    half = image.shape[1]
    core = lax.rem(lax.axis_index("px"), 2)
    which = 1 - core if flip else core
    now = sigma[:, step : step + 1]
    coeff = jnp.sum(parts[...], axis=0)
    ev = eigenvalues[...]
    shrunk = (coeff * (ev / (ev + now * now))).astype(bf16)
    tile = min(1024, half)

    @pl.loop(0, half // tile)
    def _(i):
        at = rows_at(which * half + i * tile, tile, tile)
        image[:, rows_at(i * tile, tile, tile)] = lax.dot_general(
            shrunk, e_vmem[at, :], NT, preferred_element_type=f32
        )


def back(step, flip, parts, eigenvalues, sigma, e_vmem):
    pixels, comps = e_vmem.shape
    return call(
        functools.partial(back_kernel, step, flip),
        shape((8, pixels // 2)),
        (parts, eigenvalues, sigma, in_vmem(e_vmem)),
        flops=8 * pixels * comps,
        name=f"back_{step}_{int(flip)}",
    )


def project_half_kernel(flip, off, e_vmem, out):
    half = off.shape[1]
    core = lax.rem(lax.axis_index("px"), 2)
    which = 1 - core if flip else core
    tile = min(1024, half)

    def step(i, total):
        at = rows_at(which * half + i * tile, tile, tile)
        part = off[:, rows_at(i * tile, tile, tile)].astype(bf16)
        return total + jnp.dot(part, e_vmem[at, :], preferred_element_type=f32)

    out[...] = lax.fori_loop(0, half // tile, step, jnp.zeros(out.shape, f32))


def project_rest_kernel(off, own, e_vmem, copies):
    half = off.shape[1]
    which = 1 - lax.rem(lax.axis_index("px"), 2)
    tile = min(1024, half)

    def step(i, total):
        at = rows_at(which * half + i * tile, tile, tile)
        part = off[:, rows_at(i * tile, tile, tile)].astype(bf16)
        return total + jnp.dot(part, e_vmem[at, :], preferred_element_type=f32)

    total = lax.fori_loop(0, half // tile, step, own[...])
    for k in range(copies.shape[0]):
        copies[k] = total


def first_update_kernel(mine, theirs, offset, sigma, out):
    half = mine.shape[1]
    core = lax.rem(lax.axis_index("px"), 2)
    ratio = sigma[:, 1:2] / sigma[:, 0:1]
    image = mine[...] + theirs[...]
    out[...] = image + ratio * (offset[:, rows_at(core * half, half, half)] - image)


def second_update_kernel(mine, theirs, offset, mean, sigma, out):
    half = mine.shape[1]
    span = half // 2
    place = lax.axis_index("px")
    core = lax.rem(place, 2)
    x = lax.div(place, 2)
    ratio = sigma[:, 2:3] / sigma[:, 1:2]
    image = mine[...] + theirs[...]
    first = jnp.where(x == 0, 1.0, 0.0).astype(f32)
    mean_half = mean[:, rows_at(core * half, half, half)]
    sent = (1.0 - ratio) * image + first * (ratio * offset[...] + mean_half)
    for k in range(2):
        out[lax.rem(k + x, 2)] = sent[:, k * span : (k + 1) * span]


def norms_kernel(slab, out, folded):
    rows, pixels = slab.shape
    height, tile = 64, 512

    @pl.loop(0, rows // height)
    def _(b):
        at = rows_at(b * height, height, height)

        def step(i, total):
            part = slab[at, rows_at(i * tile, tile, tile)].astype(f32)
            for k in range(tile // 128):
                piece = part[:, k * 128 : (k + 1) * 128]
                total = total + piece * piece
            return total

        folded[at, :] = lax.fori_loop(0, pixels // tile, step, jnp.zeros((height, 128), f32))

    out[...] = jnp.sum(folded[...], axis=1)[None, :]


def dots_kernel(first, pieces, extra, slab, out):
    count, _, width = pieces.shape
    span = slab.shape[1] // count

    def step(k, total):
        part = pieces[k, :, :span].astype(bf16)
        at = rows_at(k * span, span, span)
        return total + lax.dot_general(part, slab[:, at], NT, preferred_element_type=f32)

    out[:8] = lax.fori_loop(0, count, step, jnp.zeros((8, slab.shape[0]), f32))
    if first:
        out[8:] = jnp.broadcast_to(extra[...], (8, slab.shape[0]))
    else:
        squares = jnp.sum(pieces[:, :, span:], axis=0)[:, :1]
        out[8:] = jnp.broadcast_to(squares, (8, slab.shape[0]))


def weighted_kernel(step, gathered, norms, classes, targets, sigma, slab, out, *aside):
    count, _, width = out.shape
    span = width - PAD
    both = jnp.sum(gathered[...], axis=0)
    dots = both[:8]
    if step == 0:
        norm = both[8:9]
        aside[0][...] = norm
    else:
        norm = norms[...]
        scale = jnp.sqrt(both[8:, :1] / IMAGE_POINTS + RMS_EPSILON)
        dots = dots / scale
        aside[0][...] = jnp.broadcast_to(scale, aside[0].shape)
    now = sigma[:, 2 + step : 3 + step]
    sharp = 1.0 / (2.0 * now * now * math.sqrt(IMAGE_POINTS))
    bonus = jnp.where(classes[...].astype(f32) == column(targets[...].astype(f32)), STEERING, 0.0).astype(f32)
    scores = sharp * (2.0 * dots - norm) + bonus
    peak = jnp.max(scores, axis=1, keepdims=True)
    weights = jnp.exp(scores - peak).astype(bf16)
    mass = jnp.sum(weights.astype(f32), axis=1, keepdims=True)
    lane = lax.broadcasted_iota(jnp.int32, (8, PAD), 1)
    tail = jnp.where(lane < PAD // 2, peak, mass)

    @pl.loop(0, count)
    def _(k):
        at = rows_at(k * span, span, span)
        out[k, :, :span] = jnp.dot(weights, slab[:, at], preferred_element_type=f32)
        out[k, :, span:] = tail


def combine_kernel(step, parts, state, scale, sigma, copies, *new_state):
    count, _, width = parts.shape
    span = width - PAD
    peaks = [parts[k, :, span : span + 1] for k in range(count)]
    top = functools.reduce(jnp.maximum, peaks)
    total, mass = jnp.zeros((8, span), f32), jnp.zeros((8, 1), f32)
    for k in range(count):
        factor = jnp.exp(peaks[k] - top)
        total = total + factor * parts[k, :, :span]
        mass = mass + factor * parts[k, :, span + PAD // 2 : span + PAD // 2 + 1]
    average = total / mass
    ratio = sigma[:, 3 + step : 4 + step] / sigma[:, 2 + step : 3 + step]
    current = state[...] if step == 0 else state[...] / scale[:, :1]
    update = average + ratio * (current - average)
    square = jnp.broadcast_to(jnp.sum(update * update, axis=1, keepdims=True), (8, PAD))
    if new_state:
        new_state[0][...] = update
    for k in range(count):
        copies[k, :, :span] = update
        copies[k, :, span:] = square


def squares_kernel(pieces, out):
    span = pieces.shape[2] - PAD
    out[...] = jnp.sum(pieces[:, :, span:], axis=0)


def finish_kernel(pieces, squares, out):
    count, _, width = pieces.shape
    span = width - PAD
    total = jnp.sum(squares[...], axis=0)[:, :1]
    scale = jnp.sqrt(total / IMAGE_POINTS + RMS_EPSILON)

    @pl.loop(0, count)
    def _(k):
        out[:, rows_at(k * span, span, span)] = pieces[k, :, :span] / scale


def exchange_px(x, flip):
    size = lax.axis_size("px")
    return lax.ppermute(x, "px", [(i, i ^ flip) for i in range(size)])


def swap_rows(x):
    return lax.all_to_all(x, "rows", 0, 0, tiled=True)


def to_slices(x, turn):
    rows, px = lax.axis_size("rows"), lax.axis_size("px")
    pairs = []
    for r in range(rows):
        for p in range(px):
            upper, core = divmod(p, 2)
            piece = r * px + 2 * core + (upper + turn) % 2
            pairs.append((r * px + p, (piece % rows) * px + piece // rows))
    return lax.ppermute(x, ("rows", "px"), pairs)


def shards(
    queries, pixel_mean, eigenbasis, eigenvalues, level_ids, slab, slab_classes, target_categories
):
    rows = lax.axis_size("rows")
    pixels, comps = eigenbasis.shape
    slab_rows, slab_pixels = slab.shape
    span = slab_pixels // rows
    values = eigenvalues[None, :]
    classes = slab_classes[None, :]
    targets = target_categories[None, :]
    gauss_flops = 8 * pixels * comps
    slab_flops = 16 * slab_rows * slab_pixels

    copies, offset, basis, sigma, mean = load_project(
        queries, pixel_mean[None, :], eigenbasis, level_ids, rows
    )
    parts = swap_rows(copies)
    sent = exchange_px(back(0, True, parts, values, sigma, basis), 1)
    image = back(0, False, parts, values, sigma, basis) + sent
    across = exchange_px(image, 2)
    norms = call(
        norms_kernel,
        shape((1, slab_rows)),
        (in_vmem(slab),),
        scratch=[pltpu.VMEM((slab_rows, 128), f32)],
        flops=2 * slab_rows * slab_pixels,
        name="norms",
    )
    across, norms = lax.optimization_barrier((across, norms))
    offset = call(
        first_update_kernel,
        shape((8, pixels // 2)),
        (image, across, offset, sigma),
        name="first_update",
    )
    other = exchange_px(offset, 1)
    own = call(
        functools.partial(project_half_kernel, False),
        shape((8, comps)),
        (offset, in_vmem(basis)),
        flops=gauss_flops,
        name="project_own",
    )
    copies = call(
        project_rest_kernel,
        shape((rows, 8, comps)),
        (other, own, in_vmem(basis)),
        flops=gauss_flops,
        name="project_rest",
    )
    parts = swap_rows(copies)
    sent = exchange_px(back(1, True, parts, values, sigma, basis), 1)
    mine = back(1, False, parts, values, sigma, basis)
    outgoing = call(
        second_update_kernel,
        shape((2, 8, span)),
        (mine, sent, offset, mean, sigma),
        name="second_update",
    )
    state = [to_slices(outgoing[0], 0) + to_slices(outgoing[1], 1)]
    pieces = swap_rows(jnp.broadcast_to(state[0][None], (rows, 8, span)))
    products = call(
        functools.partial(dots_kernel, True),
        shape((16, slab_rows)),
        (pieces, norms, in_vmem(slab)),
        flops=slab_flops,
        name="dots_0",
    )
    scale = None
    for step in range(2):
        gathered = lax.all_gather(products, "px")
        weighted, aside = call(
            functools.partial(weighted_kernel, step),
            [
                shape((rows, 8, span + PAD)),
                shape((1, slab_rows)) if step == 0 else shape((8, PAD)),
            ],
            (gathered, norms, classes, targets, sigma, in_vmem(slab)),
            flops=slab_flops,
            name=f"weighted_{step}",
        )
        if step == 0:
            norms = aside
        else:
            scale = aside
        parts = swap_rows(weighted)
        copies, *state = call(
            functools.partial(combine_kernel, step),
            [shape((rows, 8, span + PAD)), shape((8, span))][: 2 - step],
            (parts, *state, sigma if scale is None else scale, sigma),
            name=f"combine_{step}",
        )
        pieces = swap_rows(copies)
        if step == 0:
            products = call(
                functools.partial(dots_kernel, False),
                shape((16, slab_rows)),
                (pieces, norms, in_vmem(slab)),
                flops=slab_flops,
                name="dots_1",
            )
    squares = call(squares_kernel, shape((8, PAD)), (pieces,), name="squares")
    squares = lax.all_gather(squares, "px")
    return call(finish_kernel, shape((8, slab_pixels)), (pieces, squares), name="finish")


def solution(mesh):
    in_specs = (
        P(None, "rows"),
        P("rows"),
        P("rows", "px"),
        P("px"),
        P(),
        P("rows", "px"),
        P("rows"),
        P(),
    )
    out_specs = P(None, "px")
    return jax.shard_map(shards, mesh=mesh, in_specs=in_specs, out_specs=out_specs, check_vma=False)
```

```python
import functools
import math

import jax
import jax.numpy as jnp
from jax import lax
from jax.experimental import pallas as pl
from jax.experimental.pallas import tpu as pltpu
from jax.sharding import PartitionSpec as P

IMAGE_POINTS = 65536
LEVELS = 64
STEERING = 1.5
RMS_EPSILON = 1e-06
MIB = 1024 * 1024
NT = (((1,), (1,)), ((), ()))
CHUNKS = 8
PAD = 128

f32 = jnp.float32
bf16 = jnp.bfloat16


def vmem():
    return pl.BlockSpec(memory_space=pltpu.VMEM)


def anywhere():
    return pl.BlockSpec(memory_space=pl.ANY)


def in_vmem(x):
    return pltpu.with_memory_space_constraint(x, pltpu.VMEM)


def shape(dims, dtype=f32):
    return jax.ShapeDtypeStruct(dims, dtype)


def call(kernel, out_shape, args, in_specs=None, scratch=(), flops=0, name=None):
    many = isinstance(out_shape, (list, tuple))
    return pl.pallas_call(
        kernel,
        in_specs=in_specs or [vmem()] * len(args),
        out_specs=[vmem()] * len(out_shape) if many else vmem(),
        out_shape=out_shape,
        scratch_shapes=list(scratch),
        compiler_params=pltpu.CompilerParams(vmem_limit_bytes=10 * MIB),
        cost_estimate=pl.CostEstimate(
            flops=flops, bytes_accessed=16 * MIB if flops else MIB, transcendentals=0
        ),
        name=name,
    )(*args)


def rows_at(start, count, unit):
    return pl.ds(pl.multiple_of(start, unit), count)


def column(row):
    count = row.shape[1]
    down = lax.broadcasted_iota(jnp.int32, (count, count), 0)
    across = lax.broadcasted_iota(jnp.int32, (count, count), 1)
    return jnp.sum(jnp.where(down == across, row, 0.0), axis=1, keepdims=True)


def load_project_kernel(
    q_hbm, mean_hbm, e_hbm, levels, copies, offset, e_vmem, sigma, mean, q, sems
):
    pixels = e_hbm.shape[0]
    chunk = pixels // CHUNKS

    def moves(c):
        at = rows_at(c * chunk, chunk, chunk)
        return (
            pltpu.make_async_copy(q_hbm.at[:, at], q.at[:, at], sems.at[c, 0]),
            pltpu.make_async_copy(mean_hbm.at[:, at], mean.at[:, at], sems.at[c, 1]),
            pltpu.make_async_copy(e_hbm.at[at], e_vmem.at[at], sems.at[c, 2]),
        )

    @pl.loop(0, CHUNKS)
    def _(c):
        for move in moves(c):
            move.start()

    lane = lax.broadcasted_iota(jnp.int32, sigma.shape, 1)
    table = jnp.zeros(sigma.shape, f32)
    for t in range(levels.shape[0]):
        fraction = column(levels[t : t + 1, :].astype(f32)) / (LEVELS - 1)
        table = jnp.where(lane == t, 0.6 * jnp.exp2(fraction), table)
    sigma[...] = table

    def step(c, total):
        for move in moves(c):
            move.wait()
        at = rows_at(c * chunk, chunk, chunk)
        off = q[:, at] - mean[:, at]
        offset[:, at] = off
        return total + jnp.dot(off.astype(bf16), e_vmem[at, :], preferred_element_type=f32)

    total = lax.fori_loop(0, CHUNKS, step, jnp.zeros((8, e_hbm.shape[1]), f32))
    for k in range(copies.shape[0]):
        copies[k] = total


def load_project(queries, mean, basis, levels, row_count):
    pixels, comps = basis.shape
    queries, mean, basis = [
        pltpu.with_memory_space_constraint(x, pltpu.HBM) for x in (queries, mean, basis)
    ]
    return call(
        load_project_kernel,
        [
            shape((row_count, 8, comps)),
            shape((8, pixels)),
            pltpu.VMEM((pixels, comps), bf16),
            shape((8, PAD)),
            shape((1, pixels)),
        ],
        (queries, mean, basis, levels),
        in_specs=[anywhere()] * 3 + [vmem()],
        scratch=[
            pltpu.VMEM((8, pixels), f32),
            pltpu.SemaphoreType.DMA((CHUNKS, 3)),
        ],
        flops=16 * pixels * comps,
        name="load_project",
    )


def back_kernel(step, flip, parts, eigenvalues, sigma, e_vmem, image):
    half = image.shape[1]
    core = lax.rem(lax.axis_index("px"), 2)
    which = 1 - core if flip else core
    now = sigma[:, step : step + 1]
    coeff = jnp.sum(parts[...], axis=0)
    ev = eigenvalues[...]
    shrunk = (coeff * (ev / (ev + now * now))).astype(bf16)
    tile = min(1024, half)

    @pl.loop(0, half // tile)
    def _(i):
        at = rows_at(which * half + i * tile, tile, tile)
        image[:, rows_at(i * tile, tile, tile)] = lax.dot_general(
            shrunk, e_vmem[at, :], NT, preferred_element_type=f32
        )


def back(step, flip, parts, eigenvalues, sigma, e_vmem):
    pixels, comps = e_vmem.shape
    return call(
        functools.partial(back_kernel, step, flip),
        shape((8, pixels // 2)),
        (parts, eigenvalues, sigma, in_vmem(e_vmem)),
        flops=8 * pixels * comps,
        name=f"back_{step}_{int(flip)}",
    )


def project_half_kernel(flip, off, e_vmem, out):
    half = off.shape[1]
    core = lax.rem(lax.axis_index("px"), 2)
    which = 1 - core if flip else core
    tile = min(1024, half)

    def step(i, total):
        at = rows_at(which * half + i * tile, tile, tile)
        part = off[:, rows_at(i * tile, tile, tile)].astype(bf16)
        return total + jnp.dot(part, e_vmem[at, :], preferred_element_type=f32)

    out[...] = lax.fori_loop(0, half // tile, step, jnp.zeros(out.shape, f32))


def project_rest_kernel(off, own, e_vmem, copies):
    half = off.shape[1]
    which = 1 - lax.rem(lax.axis_index("px"), 2)
    tile = min(1024, half)

    def step(i, total):
        at = rows_at(which * half + i * tile, tile, tile)
        part = off[:, rows_at(i * tile, tile, tile)].astype(bf16)
        return total + jnp.dot(part, e_vmem[at, :], preferred_element_type=f32)

    total = lax.fori_loop(0, half // tile, step, own[...])
    for k in range(copies.shape[0]):
        copies[k] = total


def first_update_kernel(mine, theirs, offset, sigma, out):
    half = mine.shape[1]
    core = lax.rem(lax.axis_index("px"), 2)
    ratio = sigma[:, 1:2] / sigma[:, 0:1]
    image = mine[...] + theirs[...]
    out[...] = image + ratio * (offset[:, rows_at(core * half, half, half)] - image)


def second_update_kernel(mine, theirs, offset, mean, sigma, out):
    half = mine.shape[1]
    span = half // 2
    place = lax.axis_index("px")
    core = lax.rem(place, 2)
    x = lax.div(place, 2)
    ratio = sigma[:, 2:3] / sigma[:, 1:2]
    image = mine[...] + theirs[...]
    first = jnp.where(x == 0, 1.0, 0.0).astype(f32)
    mean_half = mean[:, rows_at(core * half, half, half)]
    sent = (1.0 - ratio) * image + first * (ratio * offset[...] + mean_half)
    for k in range(2):
        out[lax.rem(k + x, 2)] = sent[:, k * span : (k + 1) * span]


def norms_kernel(slab, out, folded):
    rows, pixels = slab.shape
    height, tile = 64, 512

    @pl.loop(0, rows // height)
    def _(b):
        at = rows_at(b * height, height, height)

        def step(i, total):
            part = slab[at, rows_at(i * tile, tile, tile)].astype(f32)
            for k in range(tile // 128):
                piece = part[:, k * 128 : (k + 1) * 128]
                total = total + piece * piece
            return total

        folded[at, :] = lax.fori_loop(0, pixels // tile, step, jnp.zeros((height, 128), f32))

    out[...] = jnp.sum(folded[...], axis=1)[None, :]


def block_at(k, span):
    block = lax.bitwise_xor(lax.axis_index("rows"), k)
    return rows_at(block * span, span, span)


def dots_kernel(offsets, *refs):
    *inputs, slab, out = refs
    pieces, before = inputs[: len(offsets)], inputs[len(offsets) :]
    span = slab.shape[1] // lax.axis_size("rows")
    total = before[0][:8] if before else jnp.zeros((8, slab.shape[0]), f32)
    rest = before[0][8:] if before else jnp.zeros((8, slab.shape[0]), f32)
    for piece, ks in zip(pieces, offsets):
        for i, k in enumerate(ks):
            block = piece if len(piece.shape) == 2 else piece.at[i]
            total = total + lax.dot_general(
                block[:, :span].astype(bf16),
                slab[:, block_at(k, span)],
                NT,
                preferred_element_type=f32,
            )
            if block.shape[1] > span:
                lane = lax.broadcasted_iota(jnp.int32, rest.shape, 1)
                rest = rest + jnp.where(lane >= 0, block[:, span : span + 1], 0.0)
    out[:8] = total
    out[8:] = rest


def dots(pieces, offsets, before, slab, name):
    rows = lax.axis_size("rows")
    count = sum(len(ks) for ks in offsets)
    return call(
        functools.partial(dots_kernel, offsets),
        shape((16, slab.shape[0])),
        (*pieces, *before, in_vmem(slab)),
        flops=16 * count * slab.shape[0] * (slab.shape[1] // rows),
        name=name,
    )


def put_chunks(weights, tail, ks, slab, out):
    span = slab.shape[1] // lax.axis_size("rows")
    for i, k in enumerate(ks):
        out[i, :, :span] = jnp.dot(
            weights, slab[:, block_at(k, span)], preferred_element_type=f32
        )
        out[i, :, span:] = tail


def scores_kernel(step, ks, gathered, norms, classes, targets, sigma, slab, out, kept, tails, aside):
    both = jnp.sum(gathered[...], axis=0)
    inner = both[:8]
    if step == 0:
        norm = both[8:9]
        aside[...] = jnp.broadcast_to(norm, aside.shape)
    else:
        norm = norms[:1]
        scale = jnp.sqrt(both[8:, :1] / IMAGE_POINTS + RMS_EPSILON)
        inner = inner / scale
        aside[...] = jnp.broadcast_to(scale, aside.shape)
    now = sigma[:, 2 + step : 3 + step]
    sharp = 1.0 / (2.0 * now * now * math.sqrt(IMAGE_POINTS))
    wanted = column(targets[...].astype(f32))
    bonus = jnp.where(classes[...].astype(f32) == wanted, STEERING, 0.0).astype(f32)
    scores = sharp * (2.0 * inner - norm) + bonus
    peak = jnp.max(scores, axis=1, keepdims=True)
    weights = jnp.exp(scores - peak).astype(bf16)
    kept[...] = weights.astype(f32)
    mass = jnp.sum(weights.astype(f32), axis=1, keepdims=True)
    lane = lax.broadcasted_iota(jnp.int32, (8, PAD), 1)
    tail = jnp.where(lane < PAD // 2, peak, mass)
    tails[...] = tail
    put_chunks(weights, tail, ks, slab, out)


def chunks_kernel(ks, kept, tails, slab, out):
    put_chunks(kept[...].astype(bf16), tails[...], ks, slab, out)


def merge(parts, span):
    peaks = [part[:, span : span + 1] for part in parts]
    masses = [part[:, span + PAD // 2 : span + PAD // 2 + 1] for part in parts]
    top = functools.reduce(jnp.maximum, peaks)
    total, mass = 0.0, 0.0
    for part, peak, part_mass in zip(parts, peaks, masses):
        factor = jnp.exp(peak - top)
        total = total + factor * part[:, :span]
        mass = mass + factor * part_mass
    return top, mass, total


def merge_kernel(mine, theirs, *outs):
    span = mine.shape[2] - PAD
    lane = lax.broadcasted_iota(jnp.int32, (8, PAD), 1)
    for i, out in enumerate(outs):
        top, mass, total = merge([mine.at[i], theirs.at[i]], span)
        out[:, :span] = total
        out[:, span:] = jnp.where(lane < PAD // 2, top, mass)


def combine_kernel(step, count, *refs):
    parts = refs[:count]
    state, scale, sigma, out = refs[count:]
    span = out.shape[1] - PAD
    _, mass, total = merge(parts, span)
    average = total / mass
    ratio = sigma[:, 3 + step : 4 + step] / sigma[:, 2 + step : 3 + step]
    current = state[:, :span]
    if step:
        current = current / scale[:, :1]
    update = average + ratio * (current - average)
    out[:, :span] = update
    out[:, span:] = jnp.broadcast_to(jnp.sum(update * update, axis=1, keepdims=True), (8, PAD))


def spread(flat):
    evens = list(range(0, flat, 2))
    near, far = evens[: len(evens) // 2], evens[len(evens) // 2 :]
    return near, far


def gather_rows(state):
    rows = lax.axis_size("rows")
    near, far = spread(rows)
    got = {k: exchange("rows", state, k) if k else state for k in near + far}
    first = exchange("rows", jnp.stack([got[k] for k in near]), 1)
    second = exchange("rows", jnp.stack([got[k] for k in far]), 1)
    pieces = [got[k] for k in near + far] + [first, second]
    offsets = [(k,) for k in near + far]
    offsets += [tuple(k ^ 1 for k in near), tuple(k ^ 1 for k in far)]
    return pieces, offsets


def gather_dots(state, slab, name):
    pieces, offsets = gather_rows(state)
    evens = len(offsets) - 2
    total = dots(pieces[:1], offsets[:1], (), slab, name + "_own")
    for i, (lo, hi) in enumerate(
        ((1, evens // 2), (evens // 2, evens), (evens, evens + 1), (evens + 1, evens + 2))
    ):
        if hi > lo:
            total = dots(pieces[lo:hi], offsets[lo:hi], (total,), slab, f"{name}_{i}")
    return total


def reduce_rows(step, gathered, norms, classes, targets, sigma, slab):
    rows = lax.axis_size("rows")
    slab_rows, slab_pixels = slab.shape
    span = slab_pixels // rows
    near, far = spread(rows)
    unit = 16 * slab_rows * span

    def chunks(ks, name):
        return call(
            functools.partial(chunks_kernel, ks),
            shape((len(ks), 8, span + PAD)),
            (kept, tails, in_vmem(slab)),
            flops=unit * len(ks),
            name=f"{name}_{step}",
        )

    def merged(mine, theirs, name):
        outs = [shape((8, span + PAD))] * mine.shape[0]
        return call(merge_kernel, outs, (mine, theirs), name=f"{name}_{step}")

    ks = tuple(k ^ 1 for k in far)
    across, kept, tails, aside = call(
        functools.partial(scores_kernel, step, ks),
        [
            shape((len(ks), 8, span + PAD)),
            shape((8, slab_rows)),
            shape((8, PAD)),
            shape((8, slab_rows)),
        ],
        (gathered, norms, classes, targets, sigma, in_vmem(slab)),
        flops=unit * len(ks),
        name=f"scores_{step}",
    )
    across = exchange("rows", across, 1)
    beside = exchange("rows", chunks(tuple(k ^ 1 for k in near), "near_across"), 1)
    sent = merged(chunks(tuple(near), "near_own"), beside, "near_merge")
    parts = [exchange("rows", x, k) if k else x for x, k in zip(sent, near)]
    sent = merged(chunks(tuple(far), "far_own"), across, "far_merge")
    parts += [exchange("rows", x, k) for x, k in zip(sent, far)]
    return parts, aside


def squares_kernel(*refs):
    *pieces, out = refs
    total = jnp.zeros(out.shape, f32)
    for piece in pieces:
        span = piece.shape[-1] - PAD
        if len(piece.shape) == 2:
            total = total + piece[:, span:]
        else:
            total = total + jnp.sum(piece[:, :, span:], axis=0)
    out[...] = total


def finish_kernel(offsets, *refs):
    *pieces, squares, out = refs
    total = jnp.sum(squares[...], axis=0)[:, :1]
    scale = 1.0 / jnp.sqrt(total / IMAGE_POINTS + RMS_EPSILON)
    for piece, ks in zip(pieces, offsets):
        span = piece.shape[-1] - PAD
        for i, k in enumerate(ks):
            block = piece if len(piece.shape) == 2 else piece.at[i]
            out[:, block_at(k, span)] = block[:, :span] * scale


def exchange(axis, x, flip):
    return lax.ppermute(x, axis, [(i, i ^ flip) for i in range(lax.axis_size(axis))])


def swap_rows(x):
    return lax.all_to_all(x, "rows", 0, 0, tiled=True)


def to_slices(x, turn):
    rows, px = lax.axis_size("rows"), lax.axis_size("px")
    pairs = []
    for r in range(rows):
        for p in range(px):
            upper, core = divmod(p, 2)
            piece = r * px + 2 * core + (upper + turn) % 2
            pairs.append((r * px + p, (piece % rows) * px + piece // rows))
    return lax.ppermute(x, ("rows", "px"), pairs)


def shards(
    queries, pixel_mean, eigenbasis, eigenvalues, level_ids, slab, slab_classes, target_categories
):
    rows = lax.axis_size("rows")
    pixels, comps = eigenbasis.shape
    slab_rows, slab_pixels = slab.shape
    span = slab_pixels // rows
    values = eigenvalues[None, :]
    classes = slab_classes[None, :]
    targets = target_categories[None, :]
    gauss_flops = 8 * pixels * comps

    copies, offset, basis, sigma, mean = load_project(
        queries, pixel_mean[None, :], eigenbasis, level_ids, rows
    )
    parts = swap_rows(copies)
    sent = exchange("px", back(0, True, parts, values, sigma, basis), 1)
    image = back(0, False, parts, values, sigma, basis) + sent
    across = exchange("px", image, 2)
    norms = call(
        norms_kernel,
        shape((1, slab_rows)),
        (in_vmem(slab),),
        scratch=[pltpu.VMEM((slab_rows, 128), f32)],
        flops=2 * slab_rows * slab_pixels,
        name="norms",
    )
    across, norms = lax.optimization_barrier((across, norms))
    offset = call(
        first_update_kernel,
        shape((8, pixels // 2)),
        (image, across, offset, sigma),
        name="first_update",
    )
    other = exchange("px", offset, 1)
    own = call(
        functools.partial(project_half_kernel, False),
        shape((8, comps)),
        (offset, in_vmem(basis)),
        flops=gauss_flops,
        name="project_own",
    )
    copies = call(
        project_rest_kernel,
        shape((rows, 8, comps)),
        (other, own, in_vmem(basis)),
        flops=gauss_flops,
        name="project_rest",
    )
    parts = swap_rows(copies)
    sent = exchange("px", back(1, True, parts, values, sigma, basis), 1)
    mine = back(1, False, parts, values, sigma, basis)
    outgoing = call(
        second_update_kernel,
        shape((2, 8, span)),
        (mine, sent, offset, mean, sigma),
        name="second_update",
    )
    state = to_slices(outgoing[0], 0) + to_slices(outgoing[1], 1)
    products = gather_dots(state, slab, "dots_0")
    products = jnp.concatenate([products[:8], jnp.broadcast_to(norms, (8, slab_rows))])
    scale = norms
    for step in range(2):
        gathered = lax.all_gather(products, "px")
        parts, aside = reduce_rows(step, gathered, norms, classes, targets, sigma, slab)
        if step == 0:
            norms = aside
        else:
            scale = aside
        state = call(
            functools.partial(combine_kernel, step, len(parts)),
            shape((8, span + PAD)),
            (*parts, state, scale, sigma),
            name=f"combine_{step}",
        )
        if step == 0:
            products = gather_dots(state, slab, "dots_1")
    pieces, offsets = gather_rows(state)
    squares = call(squares_kernel, shape((8, PAD)), pieces, name="squares")
    squares = lax.all_gather(squares, "px")
    return call(
        functools.partial(finish_kernel, offsets),
        shape((8, slab_pixels)),
        (*pieces, squares),
        name="finish",
    )


def solution(mesh):
    in_specs = (
        P(None, "rows"),
        P("rows"),
        P("rows", "px"),
        P("px"),
        P(),
        P("rows", "px"),
        P("rows"),
        P(),
    )
    out_specs = P(None, "px")
    return jax.shard_map(shards, mesh=mesh, in_specs=in_specs, out_specs=out_specs, check_vma=False)
```

```python
import functools
import math

import jax
import jax.numpy as jnp
from jax import lax
from jax.experimental import pallas as pl
from jax.experimental.pallas import tpu as pltpu
from jax.sharding import PartitionSpec as P

IMAGE_POINTS = 65536
LEVELS = 64
STEERING = 1.5
RMS_EPSILON = 1e-06
MIB = 1024 * 1024
NT = (((1,), (1,)), ((), ()))
CHUNKS = 16
PAD = 128

f32 = jnp.float32
bf16 = jnp.bfloat16


def vmem():
    return pl.BlockSpec(memory_space=pltpu.VMEM)


def anywhere():
    return pl.BlockSpec(memory_space=pl.ANY)


def in_vmem(x):
    return pltpu.with_memory_space_constraint(x, pltpu.VMEM)


def shape(dims, dtype=f32):
    return jax.ShapeDtypeStruct(dims, dtype)


def call(kernel, out_shape, args, in_specs=None, scratch=(), flops=0, name=None):
    many = isinstance(out_shape, (list, tuple))
    return pl.pallas_call(
        kernel,
        in_specs=in_specs or [vmem()] * len(args),
        out_specs=[vmem()] * len(out_shape) if many else vmem(),
        out_shape=out_shape,
        scratch_shapes=list(scratch),
        compiler_params=pltpu.CompilerParams(vmem_limit_bytes=10 * MIB),
        cost_estimate=pl.CostEstimate(
            flops=flops, bytes_accessed=16 * MIB if flops else MIB, transcendentals=0
        ),
        name=name,
    )(*args)


def rows_at(start, count, unit):
    return pl.ds(pl.multiple_of(start, unit), count)


def column(row):
    count = row.shape[1]
    down = lax.broadcasted_iota(jnp.int32, (count, count), 0)
    across = lax.broadcasted_iota(jnp.int32, (count, count), 1)
    return jnp.sum(jnp.where(down == across, row, 0.0), axis=1, keepdims=True)


def load_project_kernel(
    q_hbm, mean_hbm, e_hbm, levels_hbm, copies, offset, e_vmem, sigma, mean, q, levels, sems
):
    pixels = e_hbm.shape[0]
    chunk = pixels // CHUNKS

    def moves(c):
        at = rows_at(c * chunk, chunk, chunk)
        return (
            pltpu.make_async_copy(q_hbm.at[:, at], q.at[:, at], sems.at[c, 0]),
            pltpu.make_async_copy(mean_hbm.at[:, at], mean.at[:, at], sems.at[c, 1]),
            pltpu.make_async_copy(e_hbm.at[at], e_vmem.at[at], sems.at[c, 2]),
        )

    tables = pltpu.make_async_copy(levels_hbm, levels, sems.at[CHUNKS, 0])
    tables.start()

    @pl.loop(0, CHUNKS)
    def _(c):
        for move in moves(c):
            move.start()

    tables.wait()
    lane = lax.broadcasted_iota(jnp.int32, sigma.shape, 1)
    table = jnp.zeros(sigma.shape, f32)
    for t in range(levels.shape[0]):
        fraction = column(levels[t : t + 1, :].astype(f32)) / (LEVELS - 1)
        table = jnp.where(lane == t, 0.6 * jnp.exp2(fraction), table)
    sigma[...] = table

    def step(c, total):
        for move in moves(c):
            move.wait()
        at = rows_at(c * chunk, chunk, chunk)
        off = q[:, at] - mean[:, at]
        offset[:, at] = off
        return total + jnp.dot(off.astype(bf16), e_vmem[at, :], preferred_element_type=f32)

    total = lax.fori_loop(0, CHUNKS, step, jnp.zeros((8, e_hbm.shape[1]), f32))
    for k in range(copies.shape[0]):
        copies[k] = total


def load_project(queries, mean, basis, levels, row_count):
    pixels, comps = basis.shape
    queries, mean, basis, levels = [
        pltpu.with_memory_space_constraint(x, pltpu.HBM) for x in (queries, mean, basis, levels)
    ]
    return call(
        load_project_kernel,
        [
            shape((row_count, 8, comps)),
            shape((8, pixels)),
            pltpu.VMEM((pixels, comps), bf16),
            shape((8, PAD)),
            shape((1, pixels)),
        ],
        (queries, mean, basis, levels),
        in_specs=[anywhere()] * 4,
        scratch=[
            pltpu.VMEM((8, pixels), f32),
            pltpu.VMEM(levels.shape, jnp.int32),
            pltpu.SemaphoreType.DMA((CHUNKS + 1, 3)),
        ],
        flops=16 * pixels * comps,
        name="load_project",
    )


def back_kernel(step, part, parts, eigenvalues, sigma, e_vmem, image):
    span = image.shape[1]
    place = lax.axis_index("px")
    core, upper = lax.rem(place, 2), lax.div(place, 2)
    if part == "mine":
        start = core * span
    elif part == "theirs":
        start = (1 - core) * span
    else:
        start = (2 * core + (upper if part == "keep" else 1 - upper)) * span
    now = sigma[:, step : step + 1]
    coeff = jnp.sum(parts[...], axis=0)
    ev = eigenvalues[...]
    shrunk = (coeff * (ev / (ev + now * now))).astype(bf16)
    tile = min(4096, span)

    @pl.loop(0, span // tile)
    def _(i):
        at = rows_at(start + i * tile, tile, tile)
        image[:, rows_at(i * tile, tile, tile)] = lax.dot_general(
            shrunk, e_vmem[at, :], NT, preferred_element_type=f32
        )


def back(step, part, parts, eigenvalues, sigma, e_vmem):
    pixels, comps = e_vmem.shape
    span = pixels // (2 if part in ("mine", "theirs") else 4)
    return call(
        functools.partial(back_kernel, step, part),
        shape((8, span)),
        (parts, eigenvalues, sigma, in_vmem(e_vmem)),
        flops=16 * span * comps,
        name=f"back_{step}_{part}",
    )


def project_half_kernel(flip, off, e_vmem, out):
    half = off.shape[1]
    core = lax.rem(lax.axis_index("px"), 2)
    which = 1 - core if flip else core
    tile = min(4096, half)

    def step(i, total):
        at = rows_at(which * half + i * tile, tile, tile)
        part = off[:, rows_at(i * tile, tile, tile)].astype(bf16)
        return total + jnp.dot(part, e_vmem[at, :], preferred_element_type=f32)

    out[...] = lax.fori_loop(0, half // tile, step, jnp.zeros(out.shape, f32))


def project_rest_kernel(off, own, e_vmem, copies):
    half = off.shape[1]
    which = 1 - lax.rem(lax.axis_index("px"), 2)
    tile = min(4096, half)

    def step(i, total):
        at = rows_at(which * half + i * tile, tile, tile)
        part = off[:, rows_at(i * tile, tile, tile)].astype(bf16)
        return total + jnp.dot(part, e_vmem[at, :], preferred_element_type=f32)

    total = lax.fori_loop(0, half // tile, step, own[...])
    for k in range(copies.shape[0]):
        copies[k] = total


def first_update_kernel(mine, theirs, offset, sigma, out):
    half = mine.shape[1]
    core = lax.rem(lax.axis_index("px"), 2)
    ratio = sigma[:, 1:2] / sigma[:, 0:1]
    image = mine[...] + theirs[...]
    out[...] = image + ratio * (offset[:, rows_at(core * half, half, half)] - image)


def give_kernel(image, other, out):
    span = image.shape[1]
    upper = lax.div(lax.axis_index("px"), 2)
    out[...] = image[...] + other[:, rows_at((1 - upper) * span, span, span)]


def second_update_kernel(image, other, given, offset, mean, sigma, out):
    span = image.shape[1]
    place = lax.axis_index("px")
    core, upper = lax.rem(place, 2), lax.div(place, 2)
    ratio = sigma[:, 2:3] / sigma[:, 1:2]
    at = rows_at(upper * span, span, span)
    total = image[...] + other[:, at] + given[...]
    average = mean[:, rows_at((2 * core + upper) * span, span, span)]
    out[...] = average + total + ratio * (offset[:, at] - total)


def norms_kernel(slab, out, folded):
    rows, pixels = slab.shape
    height, tile = 64, 512

    @pl.loop(0, rows // height)
    def _(b):
        at = rows_at(b * height, height, height)

        def step(i, total):
            part = slab[at, rows_at(i * tile, tile, tile)].astype(f32)
            for k in range(tile // 128):
                piece = part[:, k * 128 : (k + 1) * 128]
                total = total + piece * piece
            return total

        folded[at, :] = lax.fori_loop(0, pixels // tile, step, jnp.zeros((height, 128), f32))

    out[...] = jnp.sum(folded[...], axis=1)[None, :]


def block_at(k, span):
    px = lax.axis_size("px")
    per = lax.axis_size("rows") // px
    other = lax.bitwise_xor(lax.axis_index("rows"), k)
    return rows_at((lax.rem(other, per) * px + lax.div(other, per)) * span, span, span)


def dots_kernel(offsets, fresh, *refs):
    *inputs, slab, out = refs
    pieces, before = inputs[: len(offsets)], inputs[len(offsets) :]
    span = slab.shape[1] // lax.axis_size("rows")
    total = before[0][:8] if before and not fresh else jnp.zeros((8, slab.shape[0]), f32)
    rest = before[0][8:] if before else jnp.zeros((8, slab.shape[0]), f32)
    for piece, ks in zip(pieces, offsets):
        for i, k in enumerate(ks):
            block = piece if len(piece.shape) == 2 else piece.at[i]
            total = total + lax.dot_general(
                block[:, :span].astype(bf16),
                slab[:, block_at(k, span)],
                NT,
                preferred_element_type=f32,
            )
            if block.shape[1] > span:
                lane = lax.broadcasted_iota(jnp.int32, rest.shape, 1)
                rest = rest + jnp.where(lane >= 0, block[:, span : span + 1], 0.0)
    out[:8] = total
    out[8:] = rest


def dots(pieces, offsets, before, slab, name, fresh=False):
    rows = lax.axis_size("rows")
    count = sum(len(ks) for ks in offsets)
    return call(
        functools.partial(dots_kernel, offsets, fresh),
        shape((16, slab.shape[0])),
        (*pieces, *before, in_vmem(slab)),
        flops=16 * count * slab.shape[0] * (slab.shape[1] // rows),
        name=name,
    )


def read_slices(piece, norms, slab):
    rows, px = lax.axis_size("rows"), lax.axis_size("px")
    per = rows // px
    got = [to_readers(piece, turn) for turn in range(px)]
    halves = [range(px // 2), range(px // 2, px)]
    packs = [jnp.stack([got[t] for t in half]) for half in halves]
    groups = [([got[t] for t in half], [(t * per,) for t in half]) for half in halves]
    for k in range(1, per):
        for pack, half in zip(packs, halves):
            groups.append(([exchange("rows", pack, k)], [tuple(t * per ^ k for t in half)]))
    total = (jnp.broadcast_to(norms, (16, slab.shape[0])),)
    for i, (pieces, offsets) in enumerate(groups):
        total = (dots(pieces, offsets, total, slab, f"dots_0_{i}", i == 0),)
    return got[0], total[0]


def put_chunks(weights, tail, ks, slab, out):
    span = slab.shape[1] // lax.axis_size("rows")
    for i, k in enumerate(ks):
        out[i, :, :span] = jnp.dot(
            weights, slab[:, block_at(k, span)], preferred_element_type=f32
        )
        out[i, :, span:] = tail


def scores_kernel(step, ks, gathered, norms, classes, targets, sigma, slab, out, kept, tails, aside):
    both = jnp.sum(gathered[...], axis=0)
    inner = both[:8]
    if step == 0:
        norm = both[8:9]
        aside[...] = jnp.broadcast_to(norm, aside.shape)
    else:
        norm = norms[:1]
        scale = jnp.sqrt(both[8:, :1] / IMAGE_POINTS + RMS_EPSILON)
        inner = inner / scale
        aside[...] = jnp.broadcast_to(scale, aside.shape)
    now = sigma[:, 2 + step : 3 + step]
    sharp = 1.0 / (2.0 * now * now * math.sqrt(IMAGE_POINTS))
    wanted = column(targets[...].astype(f32))
    bonus = jnp.where(classes[...].astype(f32) == wanted, STEERING, 0.0).astype(f32)
    scores = sharp * (2.0 * inner - norm) + bonus
    peak = jnp.max(scores, axis=1, keepdims=True)
    weights = jnp.exp(scores - peak).astype(bf16)
    kept[...] = weights.astype(f32)
    mass = jnp.sum(weights.astype(f32), axis=1, keepdims=True)
    lane = lax.broadcasted_iota(jnp.int32, (8, PAD), 1)
    tail = jnp.where(lane < PAD // 2, peak, mass)
    tails[...] = tail
    put_chunks(weights, tail, ks, slab, out)


def chunks_kernel(ks, kept, tails, slab, out):
    put_chunks(kept[...].astype(bf16), tails[...], ks, slab, out)


def merge(parts, span):
    peaks = [part[:, span : span + 1] for part in parts]
    masses = [part[:, span + PAD // 2 : span + PAD // 2 + 1] for part in parts]
    top = functools.reduce(jnp.maximum, peaks)
    total, mass = 0.0, 0.0
    for part, peak, part_mass in zip(parts, peaks, masses):
        factor = jnp.exp(peak - top)
        total = total + factor * part[:, :span]
        mass = mass + factor * part_mass
    return top, mass, total


def merge_kernel(mine, theirs, *outs):
    span = mine.shape[2] - PAD
    lane = lax.broadcasted_iota(jnp.int32, (8, PAD), 1)
    for i, out in enumerate(outs):
        top, mass, total = merge([mine.at[i], theirs.at[i]], span)
        out[:, :span] = total
        out[:, span:] = jnp.where(lane < PAD // 2, top, mass)


def combine_kernel(step, count, *refs):
    parts = refs[:count]
    state, scale, sigma, out = refs[count:]
    span = out.shape[1] - PAD
    _, mass, total = merge(parts, span)
    average = total / mass
    ratio = sigma[:, 3 + step : 4 + step] / sigma[:, 2 + step : 3 + step]
    current = state[:, :span]
    if step:
        current = current / scale[:, :1]
    update = average + ratio * (current - average)
    out[:, :span] = update
    out[:, span:] = jnp.broadcast_to(jnp.sum(update * update, axis=1, keepdims=True), (8, PAD))


def spread(flat):
    evens = list(range(0, flat, 2))
    near, far = evens[: len(evens) // 2], evens[len(evens) // 2 :]
    return near, far


def gather_rows(state):
    rows = lax.axis_size("rows")
    near, far = spread(rows)
    got = {k: exchange("rows", state, k) if k else state for k in near + far}
    first = exchange("rows", jnp.stack([got[k] for k in near]), 1)
    second = exchange("rows", jnp.stack([got[k] for k in far]), 1)
    pieces = [got[k] for k in near + far] + [first, second]
    offsets = [(k,) for k in near + far]
    offsets += [tuple(k ^ 1 for k in near), tuple(k ^ 1 for k in far)]
    return pieces, offsets


def gather_dots(state, slab, name):
    pieces, offsets = gather_rows(state)
    evens = len(offsets) - 2
    total = dots(pieces[:1], offsets[:1], (), slab, name + "_own")
    for i, (lo, hi) in enumerate(
        ((1, evens // 2), (evens // 2, evens), (evens, evens + 1), (evens + 1, evens + 2))
    ):
        if hi > lo:
            total = dots(pieces[lo:hi], offsets[lo:hi], (total,), slab, f"{name}_{i}")
    return total


def reduce_rows(step, gathered, norms, classes, targets, sigma, slab):
    rows = lax.axis_size("rows")
    slab_rows, slab_pixels = slab.shape
    span = slab_pixels // rows
    near, far = spread(rows)
    unit = 16 * slab_rows * span

    def chunks(ks, name):
        return call(
            functools.partial(chunks_kernel, ks),
            shape((len(ks), 8, span + PAD)),
            (kept, tails, in_vmem(slab)),
            flops=unit * len(ks),
            name=f"{name}_{step}",
        )

    def merged(mine, theirs, name):
        outs = [shape((8, span + PAD))] * mine.shape[0]
        return call(merge_kernel, outs, (mine, theirs), name=f"{name}_{step}")

    ks = tuple(k ^ 1 for k in far)
    across, kept, tails, aside = call(
        functools.partial(scores_kernel, step, ks),
        [
            shape((len(ks), 8, span + PAD)),
            shape((8, slab_rows)),
            shape((8, PAD)),
            shape((8, slab_rows)),
        ],
        (gathered, norms, classes, targets, sigma, in_vmem(slab)),
        flops=unit * len(ks),
        name=f"scores_{step}",
    )
    across = exchange("rows", across, 1)
    beside = exchange("rows", chunks(tuple(k ^ 1 for k in near), "near_across"), 1)
    sent = merged(chunks(tuple(near), "near_own"), beside, "near_merge")
    parts = [exchange("rows", x, k) if k else x for x, k in zip(sent, near)]
    sent = merged(chunks(tuple(far), "far_own"), across, "far_merge")
    parts += [exchange("rows", x, k) for x, k in zip(sent, far)]
    return parts, aside


def squares_kernel(*refs):
    *pieces, out = refs
    total = jnp.zeros(out.shape, f32)
    for piece in pieces:
        span = piece.shape[-1] - PAD
        if len(piece.shape) == 2:
            total = total + piece[:, span:]
        else:
            total = total + jnp.sum(piece[:, :, span:], axis=0)
    out[...] = total


def finish_kernel(offsets, *refs):
    *pieces, squares, out = refs
    total = jnp.sum(squares[...], axis=0)[:, :1]
    scale = 1.0 / jnp.sqrt(total / IMAGE_POINTS + RMS_EPSILON)
    for piece, ks in zip(pieces, offsets):
        span = piece.shape[-1] - PAD
        for i, k in enumerate(ks):
            block = piece if len(piece.shape) == 2 else piece.at[i]
            out[:, block_at(k, span)] = block[:, :span] * scale


def exchange(axis, x, flip):
    return lax.ppermute(x, axis, [(i, i ^ flip) for i in range(lax.axis_size(axis))])


def swap_rows(x):
    return lax.all_to_all(x, "rows", 0, 0, tiled=True)


def to_readers(x, turn):
    rows, px = lax.axis_size("rows"), lax.axis_size("px")
    per = rows // px
    pairs = []
    for r in range(rows):
        for p in range(px):
            upper, core = divmod(p, 2)
            place = (2 * core + upper) ^ turn
            pairs.append((r * px + p, (place * per + r % per) * px + r // per))
    return lax.ppermute(x, ("rows", "px"), pairs)


def shards(
    queries, pixel_mean, eigenbasis, eigenvalues, level_ids, slab, slab_classes, target_categories
):
    rows = lax.axis_size("rows")
    pixels, comps = eigenbasis.shape
    slab_rows, slab_pixels = slab.shape
    span = slab_pixels // rows
    values = eigenvalues[None, :]
    classes = slab_classes[None, :]
    targets = target_categories[None, :]
    gauss_flops = 8 * pixels * comps

    copies, offset, basis, sigma, mean = load_project(
        queries, pixel_mean[None, :], eigenbasis, level_ids, rows
    )
    parts = swap_rows(copies)
    sent = exchange("px", back(0, "theirs", parts, values, sigma, basis), 1)
    image = back(0, "mine", parts, values, sigma, basis) + sent
    across = exchange("px", image, 2)
    norms = call(
        norms_kernel,
        shape((1, slab_rows)),
        (in_vmem(slab),),
        scratch=[pltpu.VMEM((slab_rows, 128), f32)],
        flops=2 * slab_rows * slab_pixels,
        name="norms",
    )
    across, norms = lax.optimization_barrier((across, norms))
    offset = call(
        first_update_kernel,
        shape((8, pixels // 2)),
        (image, across, offset, sigma),
        name="first_update",
    )
    other = exchange("px", offset, 1)
    own = call(
        functools.partial(project_half_kernel, False),
        shape((8, comps)),
        (offset, in_vmem(basis)),
        flops=gauss_flops,
        name="project_own",
    )
    copies = call(
        project_rest_kernel,
        shape((rows, 8, comps)),
        (other, own, in_vmem(basis)),
        flops=gauss_flops,
        name="project_rest",
    )
    parts = swap_rows(copies)
    sent = exchange("px", back(1, "theirs", parts, values, sigma, basis), 1)
    given = call(
        give_kernel,
        shape((8, pixels // 4)),
        (back(1, "give", parts, values, sigma, basis), sent),
        name="give",
    )
    given = exchange("px", given, 2)
    piece = call(
        second_update_kernel,
        shape((8, pixels // 4)),
        (back(1, "keep", parts, values, sigma, basis), sent, given, offset, mean, sigma),
        name="second_update",
    )
    state, products = read_slices(piece, norms, slab)
    scale = norms
    for step in range(2):
        gathered = lax.all_gather(products, "px")
        parts, aside = reduce_rows(step, gathered, norms, classes, targets, sigma, slab)
        if step == 0:
            norms = aside
        else:
            scale = aside
        state = call(
            functools.partial(combine_kernel, step, len(parts)),
            shape((8, span + PAD)),
            (*parts, state, scale, sigma),
            name=f"combine_{step}",
        )
        if step == 0:
            products = gather_dots(state, slab, "dots_1")
    pieces, offsets = gather_rows(state)
    squares = call(squares_kernel, shape((8, PAD)), pieces, name="squares")
    squares = lax.all_gather(squares, "px")
    return call(
        functools.partial(finish_kernel, offsets),
        shape((8, slab_pixels)),
        (*pieces, squares),
        name="finish",
    )


def solution(mesh):
    in_specs = (
        P(None, "rows"),
        P("rows"),
        P("rows", "px"),
        P("px"),
        P(),
        P("rows", "px"),
        P("rows"),
        P(),
    )
    out_specs = P(None, "px")
    return jax.shard_map(shards, mesh=mesh, in_specs=in_specs, out_specs=out_specs, check_vma=False)
```

```python
import functools
import math

import jax
import jax.numpy as jnp
from jax import lax
from jax.experimental import pallas as pl
from jax.experimental.pallas import tpu as pltpu
from jax.sharding import PartitionSpec as P

IMAGE_POINTS = 65536
LEVELS = 64
STEERING = 1.5
RMS_EPSILON = 1e-06
MIB = 1024 * 1024
NT = (((1,), (1,)), ((), ()))
CHUNKS = 16
PAD = 128

f32 = jnp.float32
bf16 = jnp.bfloat16


def vmem():
    return pl.BlockSpec(memory_space=pltpu.VMEM)


def anywhere():
    return pl.BlockSpec(memory_space=pl.ANY)


def in_vmem(x):
    return pltpu.with_memory_space_constraint(x, pltpu.VMEM)


def shape(dims, dtype=f32):
    return jax.ShapeDtypeStruct(dims, dtype)


def call(kernel, out_shape, args, in_specs=None, scratch=(), flops=0, name=None):
    many = isinstance(out_shape, (list, tuple))
    return pl.pallas_call(
        kernel,
        in_specs=in_specs or [vmem()] * len(args),
        out_specs=[vmem()] * len(out_shape) if many else vmem(),
        out_shape=out_shape,
        scratch_shapes=list(scratch),
        compiler_params=pltpu.CompilerParams(vmem_limit_bytes=10 * MIB),
        cost_estimate=pl.CostEstimate(
            flops=flops, bytes_accessed=16 * MIB if flops else MIB, transcendentals=0
        ),
        name=name,
    )(*args)


def rows_at(start, count, unit):
    return pl.ds(pl.multiple_of(start, unit), count)


def column(row):
    count = row.shape[1]
    down = lax.broadcasted_iota(jnp.int32, (count, count), 0)
    across = lax.broadcasted_iota(jnp.int32, (count, count), 1)
    return jnp.sum(jnp.where(down == across, row, 0.0), axis=1, keepdims=True)


def load_project_kernel(
    q_hbm, mean_hbm, e_hbm, levels_hbm, copies, offset, e_vmem, sigma, mean, q, levels, sems
):
    pixels = e_hbm.shape[0]
    chunk = pixels // CHUNKS

    def moves(c):
        at = rows_at(c * chunk, chunk, chunk)
        return (
            pltpu.make_async_copy(q_hbm.at[:, at], q.at[:, at], sems.at[c, 0]),
            pltpu.make_async_copy(mean_hbm.at[:, at], mean.at[:, at], sems.at[c, 1]),
            pltpu.make_async_copy(e_hbm.at[at], e_vmem.at[at], sems.at[c, 2]),
        )

    tables = pltpu.make_async_copy(levels_hbm, levels, sems.at[CHUNKS, 0])
    tables.start()

    @pl.loop(0, CHUNKS)
    def _(c):
        for move in moves(c):
            move.start()

    tables.wait()
    lane = lax.broadcasted_iota(jnp.int32, sigma.shape, 1)
    table = jnp.zeros(sigma.shape, f32)
    for t in range(levels.shape[0]):
        fraction = column(levels[t : t + 1, :].astype(f32)) / (LEVELS - 1)
        table = jnp.where(lane == t, 0.6 * jnp.exp2(fraction), table)
    sigma[...] = table

    def step(c, total):
        for move in moves(c):
            move.wait()
        at = rows_at(c * chunk, chunk, chunk)
        off = q[:, at] - mean[:, at]
        offset[:, at] = off
        return total + jnp.dot(off.astype(bf16), e_vmem[at, :], preferred_element_type=f32)

    total = lax.fori_loop(0, CHUNKS, step, jnp.zeros((8, e_hbm.shape[1]), f32))
    copies[...] = total


def load_project(queries, mean, basis, levels):
    pixels, comps = basis.shape
    queries, mean, basis, levels = [
        pltpu.with_memory_space_constraint(x, pltpu.HBM) for x in (queries, mean, basis, levels)
    ]
    return call(
        load_project_kernel,
        [
            shape((8, comps)),
            shape((8, pixels)),
            pltpu.VMEM((pixels, comps), bf16),
            shape((8, PAD)),
            shape((1, pixels)),
        ],
        (queries, mean, basis, levels),
        in_specs=[anywhere()] * 4,
        scratch=[
            pltpu.VMEM((8, pixels), f32),
            pltpu.VMEM(levels.shape, jnp.int32),
            pltpu.SemaphoreType.DMA((CHUNKS + 1, 3)),
        ],
        flops=16 * pixels * comps,
        name="load_project",
    )


def back_kernel(step, part, parts, eigenvalues, sigma, e_vmem, image):
    span = image.shape[1]
    place = lax.axis_index("px")
    core, upper = lax.rem(place, 2), lax.div(place, 2)
    if part == "mine":
        start = core * span
    elif part == "theirs":
        start = (1 - core) * span
    else:
        whose, which = part
        side = core if whose == "mine" else 1 - core
        start = (2 * side + (upper if which == "keep" else 1 - upper)) * span
    now = sigma[:, step : step + 1]
    coeff = jnp.sum(parts[...], axis=0)
    ev = eigenvalues[...]
    shrunk = (coeff * (ev / (ev + now * now))).astype(bf16)
    tile = min(4096, span)

    @pl.loop(0, span // tile)
    def _(i):
        at = rows_at(start + i * tile, tile, tile)
        image[:, rows_at(i * tile, tile, tile)] = lax.dot_general(
            shrunk, e_vmem[at, :], NT, preferred_element_type=f32
        )


def back(step, part, parts, eigenvalues, sigma, e_vmem):
    pixels, comps = e_vmem.shape
    span = pixels // (2 if isinstance(part, str) else 4)
    return call(
        functools.partial(back_kernel, step, part),
        shape((8, span)),
        (parts, eigenvalues, sigma, in_vmem(e_vmem)),
        flops=16 * span * comps,
        name=f"back_{step}_" + (part if isinstance(part, str) else "_".join(part)),
    )


def project_half_kernel(flip, off, e_vmem, out):
    half = off.shape[1]
    core = lax.rem(lax.axis_index("px"), 2)
    which = 1 - core if flip else core
    tile = min(4096, half)

    def step(i, total):
        at = rows_at(which * half + i * tile, tile, tile)
        part = off[:, rows_at(i * tile, tile, tile)].astype(bf16)
        return total + jnp.dot(part, e_vmem[at, :], preferred_element_type=f32)

    out[...] = lax.fori_loop(0, half // tile, step, jnp.zeros(out.shape, f32))


def project_rest_kernel(off, own, e_vmem, copies):
    half = off.shape[1]
    which = 1 - lax.rem(lax.axis_index("px"), 2)
    tile = min(4096, half)

    def step(i, total):
        at = rows_at(which * half + i * tile, tile, tile)
        part = off[:, rows_at(i * tile, tile, tile)].astype(bf16)
        return total + jnp.dot(part, e_vmem[at, :], preferred_element_type=f32)

    total = lax.fori_loop(0, half // tile, step, own[...])
    copies[...] = total


def first_update_kernel(mine, theirs, offset, sigma, out):
    half = mine.shape[1]
    core = lax.rem(lax.axis_index("px"), 2)
    ratio = sigma[:, 1:2] / sigma[:, 0:1]
    image = mine[...] + theirs[...]
    out[...] = image + ratio * (offset[:, rows_at(core * half, half, half)] - image)


def second_update_kernel(image, other, given, offset, mean, sigma, out):
    span = image.shape[1]
    place = lax.axis_index("px")
    core, upper = lax.rem(place, 2), lax.div(place, 2)
    ratio = sigma[:, 2:3] / sigma[:, 1:2]
    at = rows_at(upper * span, span, span)
    total = image[...] + other[...] + given[...]
    average = mean[:, rows_at((2 * core + upper) * span, span, span)]
    out[...] = average + total + ratio * (offset[:, at] - total)


def norms_kernel(slab, out, folded):
    rows, pixels = slab.shape
    height, tile = 64, 512

    @pl.loop(0, rows // height)
    def _(b):
        at = rows_at(b * height, height, height)

        def step(i, total):
            part = slab[at, rows_at(i * tile, tile, tile)].astype(f32)
            for k in range(tile // 128):
                piece = part[:, k * 128 : (k + 1) * 128]
                total = total + piece * piece
            return total

        folded[at, :] = lax.fori_loop(0, pixels // tile, step, jnp.zeros((height, 128), f32))

    out[...] = jnp.sum(folded[...], axis=1)[None, :]


def block_at(k, span):
    px = lax.axis_size("px")
    per = lax.axis_size("rows") // px
    other = lax.bitwise_xor(lax.axis_index("rows"), k)
    place = lax.div(other, per)
    place = lax.rem(place, 2) * (px // 2) + lax.div(place, 2)
    return rows_at((lax.rem(other, per) * px + place) * span, span, span)


def dots_kernel(offsets, fresh, *refs):
    *inputs, slab, out = refs
    pieces, before = inputs[: len(offsets)], inputs[len(offsets) :]
    span = slab.shape[1] // lax.axis_size("rows")
    total = before[0][:8] if before and not fresh else jnp.zeros((8, slab.shape[0]), f32)
    rest = before[0][8:] if before else jnp.zeros((8, slab.shape[0]), f32)
    for piece, ks in zip(pieces, offsets):
        for i, k in enumerate(ks):
            block = piece if len(piece.shape) == 2 else piece.at[i]
            total = total + lax.dot_general(
                block[:, :span].astype(bf16),
                slab[:, block_at(k, span)],
                NT,
                preferred_element_type=f32,
            )
            if block.shape[1] > span:
                lane = lax.broadcasted_iota(jnp.int32, rest.shape, 1)
                rest = rest + jnp.where(lane >= 0, block[:, span : span + 1], 0.0)
    out[:8] = total
    out[8:] = rest


def dots(pieces, offsets, before, slab, name, fresh=False):
    rows = lax.axis_size("rows")
    count = sum(len(ks) for ks in offsets)
    return call(
        functools.partial(dots_kernel, offsets, fresh),
        shape((16, slab.shape[0])),
        (*pieces, *before, in_vmem(slab)),
        flops=16 * count * slab.shape[0] * (slab.shape[1] // rows),
        name=name,
    )


def read_slices(piece, norms, slab):
    rows, px = lax.axis_size("rows"), lax.axis_size("px")
    per = rows // px
    got = [to_readers(piece, turn) for turn in range(px)]
    halves = [range(px // 2), range(px // 2, px)]
    packs = [jnp.stack([got[t] for t in half]) for half in halves]
    groups = [([got[t] for t in half], [(t * per,) for t in half]) for half in halves]
    for k in range(1, per):
        for pack, half in zip(packs, halves):
            groups.append(([exchange("rows", pack, k)], [tuple(t * per ^ k for t in half)]))
    total = (jnp.broadcast_to(norms, (16, slab.shape[0])),)
    for i, (pieces, offsets) in enumerate(groups):
        total = (dots(pieces, offsets, total, slab, f"dots_0_{i}", i == 0),)
    return got[0], total[0]


def put_chunks(weights, tail, ks, slab, out):
    span = slab.shape[1] // lax.axis_size("rows")
    for i, k in enumerate(ks):
        out[i, :, :span] = jnp.dot(
            weights, slab[:, block_at(k, span)], preferred_element_type=f32
        )
        out[i, :, span:] = tail


def scores_kernel(step, ks, g0, g1, g2, g3, norms, classes, targets, sigma, slab, out, kept, tails, aside):
    both = (g0[...] + g1[...]) + (g2[...] + g3[...])
    inner = both[:8]
    if step == 0:
        norm = both[8:9]
        aside[...] = jnp.broadcast_to(norm, aside.shape)
    else:
        norm = norms[:1]
        scale = jnp.sqrt(both[8:, :1] / IMAGE_POINTS + RMS_EPSILON)
        inner = inner / scale
        aside[...] = jnp.broadcast_to(scale, aside.shape)
    now = sigma[:, 2 + step : 3 + step]
    sharp = 1.0 / (2.0 * now * now * math.sqrt(IMAGE_POINTS))
    wanted = column(targets[...].astype(f32))
    bonus = jnp.where(classes[...].astype(f32) == wanted, STEERING, 0.0).astype(f32)
    scores = sharp * (2.0 * inner - norm) + bonus
    peak = jnp.max(scores, axis=1, keepdims=True)
    weights = jnp.exp(scores - peak).astype(bf16)
    kept[...] = weights.astype(f32)
    mass = jnp.sum(weights.astype(f32), axis=1, keepdims=True)
    lane = lax.broadcasted_iota(jnp.int32, (8, PAD), 1)
    tail = jnp.where(lane < PAD // 2, peak, mass)
    tails[...] = tail
    put_chunks(weights, tail, ks, slab, out)


def chunks_kernel(ks, kept, tails, slab, out):
    put_chunks(kept[...].astype(bf16), tails[...], ks, slab, out)


def merge(parts, span):
    peaks = [part[:, span : span + 1] for part in parts]
    masses = [part[:, span + PAD // 2 : span + PAD // 2 + 1] for part in parts]
    top = functools.reduce(jnp.maximum, peaks)
    total, mass = 0.0, 0.0
    for part, peak, part_mass in zip(parts, peaks, masses):
        factor = jnp.exp(peak - top)
        total = total + factor * part[:, :span]
        mass = mass + factor * part_mass
    return top, mass, total


def merge_kernel(mine, theirs, *outs):
    span = mine.shape[2] - PAD
    lane = lax.broadcasted_iota(jnp.int32, (8, PAD), 1)
    for i, out in enumerate(outs):
        top, mass, total = merge([mine.at[i], theirs.at[i]], span)
        out[:, :span] = total
        out[:, span:] = jnp.where(lane < PAD // 2, top, mass)


def combine_kernel(step, count, *refs):
    parts = refs[:count]
    state, scale, sigma, out = refs[count:]
    span = out.shape[1] - PAD
    _, mass, total = merge(parts, span)
    average = total / mass
    ratio = sigma[:, 3 + step : 4 + step] / sigma[:, 2 + step : 3 + step]
    current = state[:, :span]
    if step:
        current = current / scale[:, :1]
    update = average + ratio * (current - average)
    out[:, :span] = update
    out[:, span:] = jnp.broadcast_to(jnp.sum(update * update, axis=1, keepdims=True), (8, PAD))


def spread(flat):
    evens = list(range(0, flat, 2))
    near, far = evens[: len(evens) // 2], evens[len(evens) // 2 :]
    return near, far


def gather_rows(state):
    rows = lax.axis_size("rows")
    near, far = spread(rows)
    got = {k: exchange("rows", state, k) if k else state for k in near + far}
    first = exchange("rows", jnp.stack([got[k] for k in near]), 1)
    second = exchange("rows", jnp.stack([got[k] for k in far]), 1)
    pieces = [got[k] for k in near + far] + [first, second]
    offsets = [(k,) for k in near + far]
    offsets += [tuple(k ^ 1 for k in near), tuple(k ^ 1 for k in far)]
    return pieces, offsets


def gather_dots(state, slab, name):
    pieces, offsets = gather_rows(state)
    evens = len(offsets) - 2
    total = dots(pieces[:1], offsets[:1], (), slab, name + "_own")
    for i, (lo, hi) in enumerate(
        ((1, evens // 2), (evens // 2, evens), (evens, evens + 1), (evens + 1, evens + 2))
    ):
        if hi > lo:
            total = dots(pieces[lo:hi], offsets[lo:hi], (total,), slab, f"{name}_{i}")
    return total


def reduce_rows(step, gathered, norms, classes, targets, sigma, slab):
    rows = lax.axis_size("rows")
    slab_rows, slab_pixels = slab.shape
    span = slab_pixels // rows
    near, far = spread(rows)
    unit = 16 * slab_rows * span

    def chunks(ks, name):
        return call(
            functools.partial(chunks_kernel, ks),
            shape((len(ks), 8, span + PAD)),
            (kept, tails, in_vmem(slab)),
            flops=unit * len(ks),
            name=f"{name}_{step}",
        )

    def merged(mine, theirs, name):
        outs = [shape((8, span + PAD))] * mine.shape[0]
        return call(merge_kernel, outs, (mine, theirs), name=f"{name}_{step}")

    ks = tuple(k ^ 1 for k in far)
    across, kept, tails, aside = call(
        functools.partial(scores_kernel, step, ks),
        [
            shape((len(ks), 8, span + PAD)),
            shape((8, slab_rows)),
            shape((8, PAD)),
            shape((8, slab_rows)),
        ],
        (*gathered, norms, classes, targets, sigma, in_vmem(slab)),
        flops=unit * len(ks),
        name=f"scores_{step}",
    )
    across = exchange("rows", across, 1)
    beside = exchange("rows", chunks(tuple(k ^ 1 for k in near), "near_across"), 1)
    sent = merged(chunks(tuple(near), "near_own"), beside, "near_merge")
    parts = [exchange("rows", x, k) if k else x for x, k in zip(sent, near)]
    sent = merged(chunks(tuple(far), "far_own"), across, "far_merge")
    parts += [exchange("rows", x, k) for x, k in zip(sent, far)]
    return parts, aside


def squares_kernel(*refs):
    *pieces, out = refs
    total = jnp.zeros(out.shape, f32)
    for piece in pieces:
        span = piece.shape[-1] - PAD
        if len(piece.shape) == 2:
            total = total + piece[:, span:]
        else:
            total = total + jnp.sum(piece[:, :, span:], axis=0)
    out[...] = total


def finish_kernel(offsets, *refs):
    *pieces, squares, out = refs
    total = jnp.sum(squares[...], axis=0)[:, :1]
    scale = 1.0 / jnp.sqrt(total / IMAGE_POINTS + RMS_EPSILON)
    for piece, ks in zip(pieces, offsets):
        span = piece.shape[-1] - PAD
        for i, k in enumerate(ks):
            block = piece if len(piece.shape) == 2 else piece.at[i]
            out[:, block_at(k, span)] = block[:, :span] * scale


def exchange(axis, x, flip):
    return lax.ppermute(x, axis, [(i, i ^ flip) for i in range(lax.axis_size(axis))])


def sum_rows(x):
    rows = lax.axis_size("rows")
    mine = sum([exchange("rows", x, k) for k in range(2, rows, 2)], x)
    return jnp.stack([mine, exchange("rows", mine, 1)])


def to_readers(x, turn):
    rows, px = lax.axis_size("rows"), lax.axis_size("px")
    per = rows // px
    pairs = []
    for r in range(rows):
        for p in range(px):
            upper, core = divmod(p, 2)
            place = (2 * upper + core) ^ turn
            pairs.append((r * px + p, (place * per + r % per) * px + r // per))
    return lax.ppermute(x, ("rows", "px"), pairs)


def shards(
    queries, pixel_mean, eigenbasis, eigenvalues, level_ids, slab, slab_classes, target_categories
):
    rows = lax.axis_size("rows")
    pixels, comps = eigenbasis.shape
    slab_rows, slab_pixels = slab.shape
    span = slab_pixels // rows
    values = eigenvalues[None, :]
    classes = slab_classes[None, :]
    targets = target_categories[None, :]
    gauss_flops = 8 * pixels * comps

    copies, offset, basis, sigma, mean = load_project(
        queries, pixel_mean[None, :], eigenbasis, level_ids
    )
    parts = sum_rows(copies)
    sent = exchange("px", back(0, "theirs", parts, values, sigma, basis), 1)
    image = back(0, "mine", parts, values, sigma, basis) + sent
    across = exchange("px", image, 2)
    norms = call(
        norms_kernel,
        shape((1, slab_rows)),
        (in_vmem(slab),),
        scratch=[pltpu.VMEM((slab_rows, 128), f32)],
        flops=2 * slab_rows * slab_pixels,
        name="norms",
    )
    across, norms = lax.optimization_barrier((across, norms))
    offset = call(
        first_update_kernel,
        shape((8, pixels // 2)),
        (image, across, offset, sigma),
        name="first_update",
    )
    other = exchange("px", offset, 1)
    own = call(
        functools.partial(project_half_kernel, False),
        shape((8, comps)),
        (offset, in_vmem(basis)),
        flops=gauss_flops,
        name="project_own",
    )
    copies = call(
        project_rest_kernel,
        shape((8, comps)),
        (other, own, in_vmem(basis)),
        flops=gauss_flops,
        name="project_rest",
    )
    parts = sum_rows(copies)
    def quarter(which, parts):
        other = back(1, ("theirs", which), parts, values, sigma, basis)
        other = exchange("px", other, 1)
        return back(1, ("mine", which), parts, values, sigma, basis), other

    given, parts = lax.optimization_barrier((sum(quarter("give", parts)), parts))
    given = exchange("px", given, 2)
    piece = call(
        second_update_kernel,
        shape((8, pixels // 4)),
        (*quarter("keep", parts), given, offset, mean, sigma),
        name="second_update",
    )
    state, products = read_slices(piece, norms, slab)
    scale = norms
    for step in range(2):
        gathered = [products] + [exchange("px", products, k) for k in (2, 3, 1)]
        parts, aside = reduce_rows(step, gathered, norms, classes, targets, sigma, slab)
        if step == 0:
            norms = aside
        else:
            scale = aside
        state = call(
            functools.partial(combine_kernel, step, len(parts)),
            shape((8, span + PAD)),
            (*parts, state, scale, sigma),
            name=f"combine_{step}",
        )
        if step == 0:
            products = gather_dots(state, slab, "dots_1")
    pieces, offsets = gather_rows(state)
    squares = call(squares_kernel, shape((8, PAD)), pieces, name="squares")
    squares = jnp.stack([squares] + [exchange("px", squares, k) for k in (2, 3, 1)])
    return call(
        functools.partial(finish_kernel, offsets),
        shape((8, slab_pixels)),
        (*pieces, squares),
        name="finish",
    )


def solution(mesh):
    in_specs = (
        P(None, "rows"),
        P("rows"),
        P("rows", "px"),
        P("px"),
        P(),
        P("rows", "px"),
        P("rows"),
        P(),
    )
    out_specs = P(None, "px")
    return jax.shard_map(shards, mesh=mesh, in_specs=in_specs, out_specs=out_specs, check_vma=False)
```

```python
import functools
import math

import jax
import jax.numpy as jnp
from jax import lax
from jax.experimental import pallas as pl
from jax.experimental.pallas import tpu as pltpu
from jax.sharding import PartitionSpec as P

IMAGE_POINTS = 65536
LEVELS = 64
STEERING = 1.5
RMS_EPSILON = 1e-06
MIB = 1024 * 1024
NT = (((1,), (1,)), ((), ()))
CHUNKS = 16
PAD = 128

f32 = jnp.float32
bf16 = jnp.bfloat16


def vmem():
    return pl.BlockSpec(memory_space=pltpu.VMEM)


def anywhere():
    return pl.BlockSpec(memory_space=pl.ANY)


def in_vmem(x):
    return pltpu.with_memory_space_constraint(x, pltpu.VMEM)


def shape(dims, dtype=f32):
    return jax.ShapeDtypeStruct(dims, dtype)


def call(kernel, out_shape, args, in_specs=None, scratch=(), flops=0, name=None):
    many = isinstance(out_shape, (list, tuple))
    return pl.pallas_call(
        kernel,
        in_specs=in_specs or [vmem()] * len(args),
        out_specs=[vmem()] * len(out_shape) if many else vmem(),
        out_shape=out_shape,
        scratch_shapes=list(scratch),
        compiler_params=pltpu.CompilerParams(vmem_limit_bytes=10 * MIB),
        cost_estimate=pl.CostEstimate(
            flops=flops, bytes_accessed=16 * MIB if flops else MIB, transcendentals=0
        ),
        name=name,
    )(*args)


def rows_at(start, count, unit):
    return pl.ds(pl.multiple_of(start, unit), count)


def column(row):
    count = row.shape[1]
    down = lax.broadcasted_iota(jnp.int32, (count, count), 0)
    across = lax.broadcasted_iota(jnp.int32, (count, count), 1)
    return jnp.sum(jnp.where(down == across, row, 0.0), axis=1, keepdims=True)


def load_project_kernel(
    q_hbm, mean_hbm, e_hbm, levels_hbm, copies, offset, e_vmem, sigma, mean, q, levels, sems
):
    pixels = e_hbm.shape[0]
    chunk = pixels // CHUNKS

    def moves(c):
        at = rows_at(c * chunk, chunk, chunk)
        return (
            pltpu.make_async_copy(q_hbm.at[:, at], q.at[:, at], sems.at[c, 0]),
            pltpu.make_async_copy(mean_hbm.at[:, at], mean.at[:, at], sems.at[c, 1]),
            pltpu.make_async_copy(e_hbm.at[at], e_vmem.at[at], sems.at[c, 2]),
        )

    tables = pltpu.make_async_copy(levels_hbm, levels, sems.at[CHUNKS, 0])
    tables.start()

    @pl.loop(0, CHUNKS)
    def _(c):
        for move in moves(c):
            move.start()

    tables.wait()
    lane = lax.broadcasted_iota(jnp.int32, sigma.shape, 1)
    table = jnp.zeros(sigma.shape, f32)
    for t in range(levels.shape[0]):
        fraction = column(levels[t : t + 1, :].astype(f32)) / (LEVELS - 1)
        table = jnp.where(lane == t, 0.6 * jnp.exp2(fraction), table)
    sigma[...] = table

    def step(c, total):
        for move in moves(c):
            move.wait()
        at = rows_at(c * chunk, chunk, chunk)
        off = q[:, at] - mean[:, at]
        offset[:, at] = off
        return total + jnp.dot(off.astype(bf16), e_vmem[at, :], preferred_element_type=f32)

    total = lax.fori_loop(0, CHUNKS, step, jnp.zeros((8, e_hbm.shape[1]), f32))
    copies[...] = total


def load_project(queries, mean, basis, levels):
    pixels, comps = basis.shape
    queries, mean, basis, levels = [
        pltpu.with_memory_space_constraint(x, pltpu.HBM) for x in (queries, mean, basis, levels)
    ]
    return call(
        load_project_kernel,
        [
            shape((8, comps)),
            shape((8, pixels)),
            pltpu.VMEM((pixels, comps), bf16),
            shape((8, PAD)),
            shape((1, pixels)),
        ],
        (queries, mean, basis, levels),
        in_specs=[anywhere()] * 4,
        scratch=[
            pltpu.VMEM((8, pixels), f32),
            pltpu.VMEM(levels.shape, jnp.int32),
            pltpu.SemaphoreType.DMA((CHUNKS + 1, 3)),
        ],
        flops=16 * pixels * comps,
        name="load_project",
    )


def back_kernel(step, part, parts, eigenvalues, sigma, e_vmem, image):
    span = image.shape[1]
    place = lax.axis_index("px")
    core, upper = lax.rem(place, 2), lax.div(place, 2)
    if part == "mine":
        start = core * span
    elif part == "theirs":
        start = (1 - core) * span
    else:
        whose, which = part
        side = core if whose == "mine" else 1 - core
        start = (2 * side + (upper if which == "keep" else 1 - upper)) * span
    now = sigma[:, step : step + 1]
    coeff = jnp.sum(parts[...], axis=0)
    ev = eigenvalues[...]
    shrunk = (coeff * (ev / (ev + now * now))).astype(bf16)
    tile = min(4096, span)

    @pl.loop(0, span // tile)
    def _(i):
        at = rows_at(start + i * tile, tile, tile)
        image[:, rows_at(i * tile, tile, tile)] = lax.dot_general(
            shrunk, e_vmem[at, :], NT, preferred_element_type=f32
        )


def back(step, part, parts, eigenvalues, sigma, e_vmem):
    pixels, comps = e_vmem.shape
    span = pixels // (2 if isinstance(part, str) else 4)
    return call(
        functools.partial(back_kernel, step, part),
        shape((8, span)),
        (parts, eigenvalues, sigma, in_vmem(e_vmem)),
        flops=16 * span * comps,
        name=f"back_{step}_" + (part if isinstance(part, str) else "_".join(part)),
    )


def project_half_kernel(flip, off, e_vmem, out):
    half = off.shape[1]
    core = lax.rem(lax.axis_index("px"), 2)
    which = 1 - core if flip else core
    tile = min(4096, half)

    def step(i, total):
        at = rows_at(which * half + i * tile, tile, tile)
        part = off[:, rows_at(i * tile, tile, tile)].astype(bf16)
        return total + jnp.dot(part, e_vmem[at, :], preferred_element_type=f32)

    out[...] = lax.fori_loop(0, half // tile, step, jnp.zeros(out.shape, f32))


def project_rest_kernel(off, own, e_vmem, copies):
    half = off.shape[1]
    which = 1 - lax.rem(lax.axis_index("px"), 2)
    tile = min(4096, half)

    def step(i, total):
        at = rows_at(which * half + i * tile, tile, tile)
        part = off[:, rows_at(i * tile, tile, tile)].astype(bf16)
        return total + jnp.dot(part, e_vmem[at, :], preferred_element_type=f32)

    total = lax.fori_loop(0, half // tile, step, own[...])
    copies[...] = total


def first_update_kernel(mine, theirs, offset, sigma, out):
    half = mine.shape[1]
    core = lax.rem(lax.axis_index("px"), 2)
    ratio = sigma[:, 1:2] / sigma[:, 0:1]
    image = mine[...] + theirs[...]
    out[...] = image + ratio * (offset[:, rows_at(core * half, half, half)] - image)


def second_update_kernel(image, other, given, offset, mean, sigma, out):
    span = image.shape[1]
    place = lax.axis_index("px")
    core, upper = lax.rem(place, 2), lax.div(place, 2)
    ratio = sigma[:, 2:3] / sigma[:, 1:2]
    at = rows_at(upper * span, span, span)
    total = image[...] + other[...] + given[...]
    average = mean[:, rows_at((2 * core + upper) * span, span, span)]
    out[...] = average + total + ratio * (offset[:, at] - total)


def norms_kernel(slab, out, folded):
    rows, pixels = slab.shape
    height, tile = 64, 512

    @pl.loop(0, rows // height)
    def _(b):
        at = rows_at(b * height, height, height)

        def step(i, total):
            part = slab[at, rows_at(i * tile, tile, tile)].astype(f32)
            for k in range(tile // 128):
                piece = part[:, k * 128 : (k + 1) * 128]
                total = total + piece * piece
            return total

        folded[at, :] = lax.fori_loop(0, pixels // tile, step, jnp.zeros((height, 128), f32))

    out[...] = jnp.sum(folded[...], axis=1)[None, :]


def block_at(k, span):
    px = lax.axis_size("px")
    per = lax.axis_size("rows") // px
    other = lax.bitwise_xor(lax.axis_index("rows"), k)
    place = lax.div(other, per)
    place = lax.rem(place, 2) * (px // 2) + lax.div(place, 2)
    return rows_at((lax.rem(other, per) * px + place) * span, span, span)


def dots_kernel(offsets, fresh, *refs):
    *inputs, slab, out = refs
    pieces, before = inputs[: len(offsets)], inputs[len(offsets) :]
    span = slab.shape[1] // lax.axis_size("rows")
    total = before[0][:8] if before and not fresh else jnp.zeros((8, slab.shape[0]), f32)
    rest = before[0][8:] if before else jnp.zeros((8, slab.shape[0]), f32)
    for piece, ks in zip(pieces, offsets):
        for i, k in enumerate(ks):
            block = piece if len(piece.shape) == 2 else piece.at[i]
            total = total + lax.dot_general(
                block[:, :span].astype(bf16),
                slab[:, block_at(k, span)],
                NT,
                preferred_element_type=f32,
            )
            if block.shape[1] > span:
                lane = lax.broadcasted_iota(jnp.int32, rest.shape, 1)
                rest = rest + jnp.where(lane >= 0, block[:, span : span + 1], 0.0)
    out[:8] = total
    out[8:] = rest


def dots(pieces, offsets, before, slab, name, fresh=False):
    rows = lax.axis_size("rows")
    count = sum(len(ks) for ks in offsets)
    return call(
        functools.partial(dots_kernel, offsets, fresh),
        shape((16, slab.shape[0])),
        (*pieces, *before, in_vmem(slab)),
        flops=16 * count * slab.shape[0] * (slab.shape[1] // rows),
        name=name,
    )


def read_slices(piece, norms, slab):
    rows, px = lax.axis_size("rows"), lax.axis_size("px")
    per = rows // px
    got = [to_readers(piece, turn) for turn in range(px)]
    halves = [range(1, px, 2), range(0, px, 2)]
    packs = [jnp.stack([got[t] for t in half]) for half in halves]
    groups = [([got[t] for t in half], [(t * per,) for t in half]) for half in halves]
    for k in range(1, per):
        for pack, half in zip(packs, halves):
            groups.append(([exchange("rows", pack, k)], [tuple(t * per ^ k for t in half)]))
    total = (jnp.broadcast_to(norms, (16, slab.shape[0])),)
    for i, (pieces, offsets) in enumerate(groups):
        total = (dots(pieces, offsets, total, slab, f"dots_0_{i}", i == 0),)
    return got[0], total[0]


def put_chunks(weights, tail, ks, slab, out):
    span = slab.shape[1] // lax.axis_size("rows")
    for i, k in enumerate(ks):
        out[i, :, :span] = jnp.dot(
            weights, slab[:, block_at(k, span)], preferred_element_type=f32
        )
        out[i, :, span:] = tail


def scores_kernel(step, ks, g0, g1, g2, g3, norms, classes, targets, sigma, slab, out, kept, tails, aside):
    both = (g0[...] + g1[...]) + (g2[...] + g3[...])
    inner = both[:8]
    if step == 0:
        norm = both[8:9]
        aside[...] = jnp.broadcast_to(norm, aside.shape)
    else:
        norm = norms[:1]
        scale = jnp.sqrt(both[8:, :1] / IMAGE_POINTS + RMS_EPSILON)
        inner = inner / scale
        aside[...] = jnp.broadcast_to(scale, aside.shape)
    now = sigma[:, 2 + step : 3 + step]
    sharp = 1.0 / (2.0 * now * now * math.sqrt(IMAGE_POINTS))
    wanted = column(targets[...].astype(f32))
    bonus = jnp.where(classes[...].astype(f32) == wanted, STEERING, 0.0).astype(f32)
    scores = sharp * (2.0 * inner - norm) + bonus
    peak = jnp.max(scores, axis=1, keepdims=True)
    weights = jnp.exp(scores - peak).astype(bf16)
    kept[...] = weights.astype(f32)
    mass = jnp.sum(weights.astype(f32), axis=1, keepdims=True)
    lane = lax.broadcasted_iota(jnp.int32, (8, PAD), 1)
    tail = jnp.where(lane < PAD // 2, peak, mass)
    tails[...] = tail
    put_chunks(weights, tail, ks, slab, out)


def chunks_kernel(ks, kept, tails, slab, out):
    put_chunks(kept[...].astype(bf16), tails[...], ks, slab, out)


def merge(parts, span):
    peaks = [part[:, span : span + 1] for part in parts]
    masses = [part[:, span + PAD // 2 : span + PAD // 2 + 1] for part in parts]
    top = functools.reduce(jnp.maximum, peaks)
    total, mass = 0.0, 0.0
    for part, peak, part_mass in zip(parts, peaks, masses):
        factor = jnp.exp(peak - top)
        total = total + factor * part[:, :span]
        mass = mass + factor * part_mass
    return top, mass, total


def merge_kernel(mine, theirs, *outs):
    span = mine.shape[2] - PAD
    lane = lax.broadcasted_iota(jnp.int32, (8, PAD), 1)
    for i, out in enumerate(outs):
        top, mass, total = merge([mine.at[i], theirs.at[i]], span)
        out[:, :span] = total
        out[:, span:] = jnp.where(lane < PAD // 2, top, mass)


def combine_kernel(step, count, *refs):
    parts = refs[:count]
    state, scale, sigma, out = refs[count:]
    span = out.shape[1] - PAD
    _, mass, total = merge(parts, span)
    average = total / mass
    ratio = sigma[:, 3 + step : 4 + step] / sigma[:, 2 + step : 3 + step]
    current = state[:, :span]
    if step:
        current = current / scale[:, :1]
    update = average + ratio * (current - average)
    out[:, :span] = update
    out[:, span:] = jnp.broadcast_to(jnp.sum(update * update, axis=1, keepdims=True), (8, PAD))


def spread(flat):
    evens = list(range(0, flat, 2))
    near, far = evens[: len(evens) // 2], evens[len(evens) // 2 :]
    return near, far


def gather_rows(state):
    rows = lax.axis_size("rows")
    near, far = spread(rows)
    got = {k: exchange("rows", state, k) if k else state for k in near + far}
    one, two = near[:1] + far[:-1], near[1:] + far[-1:]
    first = exchange("rows", jnp.stack([got[k] for k in one]), 1)
    second = exchange("rows", jnp.stack([got[k] for k in two]), 1)
    pieces = [got[k] for k in near + far] + [first, second]
    offsets = [(k,) for k in near + far]
    offsets += [tuple(k ^ 1 for k in one), tuple(k ^ 1 for k in two)]
    return pieces, offsets


def gather_dots(state, slab, name):
    pieces, offsets = gather_rows(state)
    evens = len(offsets) - 2
    total = dots(pieces[:1], offsets[:1], (), slab, name + "_own")
    for i, (lo, hi) in enumerate(
        ((1, evens // 2), (evens // 2, evens), (evens, evens + 1), (evens + 1, evens + 2))
    ):
        if hi > lo:
            total = dots(pieces[lo:hi], offsets[lo:hi], (total,), slab, f"{name}_{i}")
    return total


def reduce_rows(step, gathered, norms, classes, targets, sigma, slab):
    rows = lax.axis_size("rows")
    slab_rows, slab_pixels = slab.shape
    span = slab_pixels // rows
    near, far = spread(rows)
    unit = 16 * slab_rows * span

    def chunks(ks, name):
        return call(
            functools.partial(chunks_kernel, ks),
            shape((len(ks), 8, span + PAD)),
            (kept, tails, in_vmem(slab)),
            flops=unit * len(ks),
            name=f"{name}_{step}",
        )

    def merged(mine, theirs, name):
        outs = [shape((8, span + PAD))] * mine.shape[0]
        return call(merge_kernel, outs, (mine, theirs), name=f"{name}_{step}")

    ks = tuple(k ^ 1 for k in far)
    across, kept, tails, aside = call(
        functools.partial(scores_kernel, step, ks),
        [
            shape((len(ks), 8, span + PAD)),
            shape((8, slab_rows)),
            shape((8, PAD)),
            shape((8, slab_rows)),
        ],
        (*gathered, norms, classes, targets, sigma, in_vmem(slab)),
        flops=unit * len(ks),
        name=f"scores_{step}",
    )
    across = exchange("rows", across, 1)
    beside = exchange("rows", chunks(tuple(k ^ 1 for k in near), "near_across"), 1)
    sent = merged(chunks(tuple(near), "near_own"), beside, "near_merge")
    parts = [exchange("rows", x, k) if k else x for x, k in zip(sent, near)]
    sent = merged(chunks(tuple(far), "far_own"), across, "far_merge")
    parts += [exchange("rows", x, k) for x, k in zip(sent, far)]
    return parts, aside


def squares_kernel(*refs):
    *pieces, out = refs
    total = jnp.zeros(out.shape, f32)
    for piece in pieces:
        span = piece.shape[-1] - PAD
        if len(piece.shape) == 2:
            total = total + piece[:, span:]
        else:
            total = total + jnp.sum(piece[:, :, span:], axis=0)
    out[...] = total


def finish_kernel(offsets, *refs):
    *pieces, squares, out = refs
    total = jnp.sum(squares[...], axis=0)[:, :1]
    scale = 1.0 / jnp.sqrt(total / IMAGE_POINTS + RMS_EPSILON)
    for piece, ks in zip(pieces, offsets):
        span = piece.shape[-1] - PAD
        for i, k in enumerate(ks):
            block = piece if len(piece.shape) == 2 else piece.at[i]
            out[:, block_at(k, span)] = block[:, :span] * scale


def exchange(axis, x, flip):
    return lax.ppermute(x, axis, [(i, i ^ flip) for i in range(lax.axis_size(axis))])


def sum_rows(x):
    rows = lax.axis_size("rows")
    mine = sum([exchange("rows", x, k) for k in range(2, rows, 2)], x)
    return jnp.stack([mine, exchange("rows", mine, 1)])


def to_readers(x, turn):
    rows, px = lax.axis_size("rows"), lax.axis_size("px")
    per = rows // px
    pairs = []
    for r in range(rows):
        for p in range(px):
            upper, core = divmod(p, 2)
            place = (2 * upper + core) ^ turn
            pairs.append((r * px + p, (place * per + r % per) * px + r // per))
    return lax.ppermute(x, ("rows", "px"), pairs)


def shards(
    queries, pixel_mean, eigenbasis, eigenvalues, level_ids, slab, slab_classes, target_categories
):
    rows = lax.axis_size("rows")
    pixels, comps = eigenbasis.shape
    slab_rows, slab_pixels = slab.shape
    span = slab_pixels // rows
    values = eigenvalues[None, :]
    classes = slab_classes[None, :]
    targets = target_categories[None, :]
    gauss_flops = 8 * pixels * comps

    copies, offset, basis, sigma, mean = load_project(
        queries, pixel_mean[None, :], eigenbasis, level_ids
    )
    parts = sum_rows(copies)
    sent = exchange("px", back(0, "theirs", parts, values, sigma, basis), 1)
    image = back(0, "mine", parts, values, sigma, basis) + sent
    across = exchange("px", image, 2)
    norms = call(
        norms_kernel,
        shape((1, slab_rows)),
        (in_vmem(slab),),
        scratch=[pltpu.VMEM((slab_rows, 128), f32)],
        flops=2 * slab_rows * slab_pixels,
        name="norms",
    )
    across, norms = lax.optimization_barrier((across, norms))
    offset = call(
        first_update_kernel,
        shape((8, pixels // 2)),
        (image, across, offset, sigma),
        name="first_update",
    )
    other = exchange("px", offset, 1)
    own = call(
        functools.partial(project_half_kernel, False),
        shape((8, comps)),
        (offset, in_vmem(basis)),
        flops=gauss_flops,
        name="project_own",
    )
    copies = call(
        project_rest_kernel,
        shape((8, comps)),
        (other, own, in_vmem(basis)),
        flops=gauss_flops,
        name="project_rest",
    )
    parts = sum_rows(copies)
    def quarter(which, parts):
        other = back(1, ("theirs", which), parts, values, sigma, basis)
        other = exchange("px", other, 1)
        return back(1, ("mine", which), parts, values, sigma, basis), other

    given, parts = lax.optimization_barrier((sum(quarter("give", parts)), parts))
    given = exchange("px", given, 2)
    piece = call(
        second_update_kernel,
        shape((8, pixels // 4)),
        (*quarter("keep", parts), given, offset, mean, sigma),
        name="second_update",
    )
    state, products = read_slices(piece, norms, slab)
    scale = norms
    for step in range(2):
        gathered = [products] + [exchange("px", products, k) for k in (2, 3, 1)]
        parts, aside = reduce_rows(step, gathered, norms, classes, targets, sigma, slab)
        if step == 0:
            norms = aside
        else:
            scale = aside
        state = call(
            functools.partial(combine_kernel, step, len(parts)),
            shape((8, span + PAD)),
            (*parts, state, scale, sigma),
            name=f"combine_{step}",
        )
        if step == 0:
            products = gather_dots(state, slab, "dots_1")
    pieces, offsets = gather_rows(state)
    squares = call(squares_kernel, shape((8, PAD)), pieces, name="squares")
    squares = jnp.stack([squares] + [exchange("px", squares, k) for k in (2, 3, 1)])
    return call(
        functools.partial(finish_kernel, offsets),
        shape((8, slab_pixels)),
        (*pieces, squares),
        name="finish",
    )


def solution(mesh):
    in_specs = (
        P(None, "rows"),
        P("rows"),
        P("rows", "px"),
        P("px"),
        P(),
        P("rows", "px"),
        P("rows"),
        P(),
    )
    out_specs = P(None, "px")
    return jax.shard_map(shards, mesh=mesh, in_specs=in_specs, out_specs=out_specs, check_vma=False)
```

```python
import functools
import math

import jax
import jax.numpy as jnp
from jax import lax
from jax.experimental import pallas as pl
from jax.experimental.pallas import tpu as pltpu
from jax.sharding import PartitionSpec as P

IMAGE_POINTS = 65536
LEVELS = 64
STEERING = 1.5
RMS_EPSILON = 1e-06
MIB = 1024 * 1024
NT = (((1,), (1,)), ((), ()))
CHUNKS = 16
PAD = 128

f32 = jnp.float32
bf16 = jnp.bfloat16


def vmem():
    return pl.BlockSpec(memory_space=pltpu.VMEM)


def anywhere():
    return pl.BlockSpec(memory_space=pl.ANY)


def in_vmem(x):
    return pltpu.with_memory_space_constraint(x, pltpu.VMEM)


def shape(dims, dtype=f32):
    return jax.ShapeDtypeStruct(dims, dtype)


def call(kernel, out_shape, args, in_specs=None, scratch=(), flops=0, name=None):
    many = isinstance(out_shape, (list, tuple))
    return pl.pallas_call(
        kernel,
        in_specs=in_specs or [vmem()] * len(args),
        out_specs=[vmem()] * len(out_shape) if many else vmem(),
        out_shape=out_shape,
        scratch_shapes=list(scratch),
        compiler_params=pltpu.CompilerParams(vmem_limit_bytes=4 * MIB),
        cost_estimate=pl.CostEstimate(
            flops=flops, bytes_accessed=16 * MIB if flops else MIB, transcendentals=0
        ),
        name=name,
    )(*args)


def rows_at(start, count, unit):
    return pl.ds(pl.multiple_of(start, unit), count)


def column(row):
    count = row.shape[1]
    down = lax.broadcasted_iota(jnp.int32, (count, count), 0)
    across = lax.broadcasted_iota(jnp.int32, (count, count), 1)
    return jnp.sum(jnp.where(down == across, row, 0.0), axis=1, keepdims=True)


def load_project_kernel(
    q_hbm, mean_hbm, e_hbm, levels_hbm, copies, offset, mine, theirs, sigma, mean, q, levels, sems
):
    pixels = e_hbm.shape[0]
    chunk = pixels // CHUNKS

    core = lax.rem(lax.axis_index("px"), 2)
    sides = ((core, mine), (1 - core, theirs))

    def source(side, c):
        return rows_at(side * (pixels // 2) + c * chunk, chunk, chunk)

    def move(i, c):
        side, held = sides[i]
        to = rows_at(c * chunk, chunk, chunk)
        return pltpu.make_async_copy(
            e_hbm.at[source(side, c)], held.at[to], sems.at[i * (CHUNKS // 2) + c]
        )

    small = [
        pltpu.make_async_copy(source, held, sems.at[CHUNKS + i])
        for i, (source, held) in enumerate(
            ((levels_hbm, levels), (q_hbm, q), (mean_hbm, mean))
        )
    ]
    small[1].start()
    small[2].start()
    small[0].start()

    for i in range(2):

        @pl.loop(0, CHUNKS // 2)
        def _(c, i=i):
            move(i, c).start()

    small[0].wait()
    lane = lax.broadcasted_iota(jnp.int32, sigma.shape, 1)
    table = jnp.zeros(sigma.shape, f32)
    for t in range(levels.shape[0]):
        fraction = column(levels[t : t + 1, :].astype(f32)) / (LEVELS - 1)
        table = jnp.where(lane == t, 0.6 * jnp.exp2(fraction), table)
    sigma[...] = table

    def step(i, c, total):
        side, held = sides[i]
        move(i, c).wait()
        at = source(side, c)
        off = q[:, at] - mean[:, at]
        offset[:, at] = off
        block = held[rows_at(c * chunk, chunk, chunk), :]
        return total + jnp.dot(off.astype(bf16), block, preferred_element_type=f32)

    small[1].wait()
    small[2].wait()
    total = jnp.zeros((8, e_hbm.shape[1]), f32)
    for i in range(2):
        total = lax.fori_loop(0, CHUNKS // 2, functools.partial(step, i), total)
    copies[...] = total


def load_project(queries, mean, basis, levels):
    pixels, comps = basis.shape
    queries, mean, basis, levels = [
        pltpu.with_memory_space_constraint(x, pltpu.HBM) for x in (queries, mean, basis, levels)
    ]
    return call(
        load_project_kernel,
        [
            shape((8, comps)),
            shape((8, pixels)),
            pltpu.VMEM((pixels // 2, comps), bf16),
            pltpu.VMEM((pixels // 2, comps), bf16),
            shape((8, PAD)),
            shape((1, pixels)),
        ],
        (queries, mean, basis, levels),
        in_specs=[anywhere()] * 4,
        scratch=[
            pltpu.VMEM((8, pixels), f32),
            pltpu.VMEM(levels.shape, jnp.int32),
            pltpu.SemaphoreType.DMA((CHUNKS + 3,)),
        ],
        flops=16 * pixels * comps,
        name="load_project",
    )


def turn_kernel(anchor, half, out):
    pixels = half.shape[0]
    tile = min(1024, pixels)

    @pl.loop(0, pixels // tile)
    def _(i):
        at = rows_at(i * tile, tile, tile)
        for k in range(out.shape[0] // 128):
            comps = slice(k * 128, (k + 1) * 128)
            out[comps, at] = half[at, comps].T


def turned(half, name, anchor):
    pixels, comps = half.shape
    return call(
        turn_kernel,
        pltpu.VMEM((comps, pixels), bf16),
        (anchor, in_vmem(half)),
        flops=pixels * comps,
        name=f"turn_{name}",
    )


def back_kernel(step, part, parts, eigenvalues, sigma, half, image):
    span = image.shape[1]
    now = sigma[:, step : step + 1]
    coeff = jnp.sum(parts[...], axis=0)
    ev = eigenvalues[...]
    shrunk = (coeff * (ev / (ev + now * now))).astype(bf16)
    if part == "whole":
        image[...] = jnp.dot(shrunk, half[...], preferred_element_type=f32)
    else:
        upper = lax.div(lax.axis_index("px"), 2)
        at = rows_at((upper if part == "keep" else 1 - upper) * span, span, span)
        image[...] = jnp.dot(shrunk, half[:, at], preferred_element_type=f32)


def back(step, part, parts, eigenvalues, sigma, half, name):
    comps, pixels = half.shape
    span = pixels if part == "whole" else pixels // 2
    return call(
        functools.partial(back_kernel, step, part),
        shape((8, span)),
        (parts, eigenvalues, sigma, in_vmem(half)),
        flops=16 * span * comps,
        name=f"back_{step}_{name}",
    )


def project_kernel(off, half, out):
    out[...] = jnp.dot(off[...].astype(bf16), half[...], preferred_element_type=f32)


def project_rest_kernel(off, own, half, out):
    part = lax.dot_general(off[...].astype(bf16), half[...], NT, preferred_element_type=f32)
    out[...] = own[...] + part


def first_update_kernel(mine, theirs, offset, sigma, out):
    half = mine.shape[1]
    core = lax.rem(lax.axis_index("px"), 2)
    ratio = sigma[:, 1:2] / sigma[:, 0:1]
    image = mine[...] + theirs[...]
    out[...] = image + ratio * (offset[:, rows_at(core * half, half, half)] - image)


def give_kernel(image, other, out):
    span = image.shape[1]
    upper = lax.div(lax.axis_index("px"), 2)
    out[...] = image[...] + other[:, rows_at((1 - upper) * span, span, span)]


def second_update_kernel(image, other, given, offset, mean, sigma, out):
    span = image.shape[1]
    place = lax.axis_index("px")
    core, upper = lax.rem(place, 2), lax.div(place, 2)
    ratio = sigma[:, 2:3] / sigma[:, 1:2]
    at = rows_at(upper * span, span, span)
    total = image[...] + other[:, at] + given[...]
    average = mean[:, rows_at((2 * core + upper) * span, span, span)]
    out[...] = average + total + ratio * (offset[:, at] - total)


def norms_kernel(slab, out, folded):
    rows, pixels = slab.shape
    height, tile = 64, 512

    @pl.loop(0, rows // height)
    def _(b):
        at = rows_at(b * height, height, height)

        def step(i, total):
            part = slab[at, rows_at(i * tile, tile, tile)].astype(f32)
            for k in range(tile // 128):
                piece = part[:, k * 128 : (k + 1) * 128]
                total = total + piece * piece
            return total

        folded[at, :] = lax.fori_loop(0, pixels // tile, step, jnp.zeros((height, 128), f32))

    out[...] = jnp.sum(folded[...], axis=1)[None, :]


def block_at(k, span):
    px = lax.axis_size("px")
    per = lax.axis_size("rows") // px
    other = lax.bitwise_xor(lax.axis_index("rows"), k)
    place = lax.div(other, per)
    place = lax.rem(place, 2) * (px // 2) + lax.div(place, 2)
    return rows_at((lax.rem(other, per) * px + place) * span, span, span)


def dots_kernel(offsets, fresh, *refs):
    *inputs, slab, out = refs
    pieces, before = inputs[: len(offsets)], inputs[len(offsets) :]
    span = slab.shape[1] // lax.axis_size("rows")
    total = before[0][:8] if before and not fresh else jnp.zeros((8, slab.shape[0]), f32)
    rest = before[0][8:] if before else jnp.zeros((8, slab.shape[0]), f32)
    for piece, ks in zip(pieces, offsets):
        for i, k in enumerate(ks):
            block = piece if len(piece.shape) == 2 else piece.at[i]
            total = total + lax.dot_general(
                block[:, :span].astype(bf16),
                slab[:, block_at(k, span)],
                NT,
                preferred_element_type=f32,
            )
            if block.shape[1] > span:
                lane = lax.broadcasted_iota(jnp.int32, rest.shape, 1)
                rest = rest + jnp.where(lane >= 0, block[:, span : span + 1], 0.0)
    out[:8] = total
    out[8:] = rest


def dots(pieces, offsets, before, slab, name, fresh=False):
    rows = lax.axis_size("rows")
    count = sum(len(ks) for ks in offsets)
    return call(
        functools.partial(dots_kernel, offsets, fresh),
        shape((16, slab.shape[0])),
        (*pieces, *before, in_vmem(slab)),
        flops=16 * count * slab.shape[0] * (slab.shape[1] // rows),
        name=name,
    )


def read_slices(piece, norms, slab):
    rows, px = lax.axis_size("rows"), lax.axis_size("px")
    per = rows // px
    got = [to_readers(piece, turn) for turn in range(px)]
    halves = [range(1, px, 2), range(0, px, 2)]
    packs = [jnp.stack([got[t] for t in half]) for half in halves]
    groups = [([got[t] for t in half], [(t * per,) for t in half]) for half in halves]
    for k in range(1, per):
        for pack, half in zip(packs, halves):
            groups.append(([exchange("rows", pack, k)], [tuple(t * per ^ k for t in half)]))
    total = (jnp.broadcast_to(norms, (16, slab.shape[0])),)
    for i, (pieces, offsets) in enumerate(groups):
        total = (dots(pieces, offsets, total, slab, f"dots_0_{i}", i == 0),)
    return got[0], total[0]


def put_chunks(weights, tail, ks, slab, out):
    span = slab.shape[1] // lax.axis_size("rows")
    for i, k in enumerate(ks):
        out[i, :, :span] = jnp.dot(
            weights, slab[:, block_at(k, span)], preferred_element_type=f32
        )
        out[i, :, span:] = tail


def scores_kernel(step, ks, g0, g1, g2, g3, norms, classes, targets, sigma, slab, out, kept, tails, aside):
    both = (g0[...] + g1[...]) + (g2[...] + g3[...])
    inner = both[:8]
    if step == 0:
        norm = both[8:9]
        aside[...] = jnp.broadcast_to(norm, aside.shape)
    else:
        norm = norms[:1]
        scale = jnp.sqrt(both[8:, :1] / IMAGE_POINTS + RMS_EPSILON)
        inner = inner / scale
        aside[...] = jnp.broadcast_to(scale, aside.shape)
    now = sigma[:, 2 + step : 3 + step]
    sharp = 1.0 / (2.0 * now * now * math.sqrt(IMAGE_POINTS))
    wanted = column(targets[...].astype(f32))
    bonus = jnp.where(classes[...].astype(f32) == wanted, STEERING, 0.0).astype(f32)
    scores = sharp * (2.0 * inner - norm) + bonus
    peak = jnp.max(scores, axis=1, keepdims=True)
    weights = jnp.exp(scores - peak).astype(bf16)
    kept[...] = weights.astype(f32)
    mass = jnp.sum(weights.astype(f32), axis=1, keepdims=True)
    lane = lax.broadcasted_iota(jnp.int32, (8, PAD), 1)
    tail = jnp.where(lane < PAD // 2, peak, mass)
    tails[...] = tail
    put_chunks(weights, tail, ks, slab, out)


def chunks_kernel(ks, kept, tails, slab, out):
    put_chunks(kept[...].astype(bf16), tails[...], ks, slab, out)


def merge(parts, span):
    peaks = [part[:, span : span + 1] for part in parts]
    masses = [part[:, span + PAD // 2 : span + PAD // 2 + 1] for part in parts]
    top = functools.reduce(jnp.maximum, peaks)
    total, mass = 0.0, 0.0
    for part, peak, part_mass in zip(parts, peaks, masses):
        factor = jnp.exp(peak - top)
        total = total + factor * part[:, :span]
        mass = mass + factor * part_mass
    return top, mass, total


def merge_kernel(mine, theirs, *outs):
    span = mine.shape[2] - PAD
    lane = lax.broadcasted_iota(jnp.int32, (8, PAD), 1)
    for i, out in enumerate(outs):
        top, mass, total = merge([mine.at[i], theirs.at[i]], span)
        out[:, :span] = total
        out[:, span:] = jnp.where(lane < PAD // 2, top, mass)


def combine_kernel(step, count, *refs):
    parts = refs[:count]
    state, scale, sigma, out = refs[count:]
    span = out.shape[1] - PAD
    _, mass, total = merge(parts, span)
    average = total / mass
    ratio = sigma[:, 3 + step : 4 + step] / sigma[:, 2 + step : 3 + step]
    current = state[:, :span]
    if step:
        current = current / scale[:, :1]
    update = average + ratio * (current - average)
    out[:, :span] = update
    out[:, span:] = jnp.broadcast_to(jnp.sum(update * update, axis=1, keepdims=True), (8, PAD))


def spread(flat):
    evens = list(range(0, flat, 2))
    near, far = evens[: len(evens) // 2], evens[len(evens) // 2 :]
    return near, far


def gather_rows(state):
    rows = lax.axis_size("rows")
    near, far = spread(rows)
    got = {k: exchange("rows", state, k) if k else state for k in near + far}
    one, two = near[:1] + far[:-1], near[1:] + far[-1:]
    first = exchange("rows", jnp.stack([got[k] for k in one]), 1)
    second = exchange("rows", jnp.stack([got[k] for k in two]), 1)
    pieces = [got[k] for k in near + far] + [first, second]
    offsets = [(k,) for k in near + far]
    offsets += [tuple(k ^ 1 for k in one), tuple(k ^ 1 for k in two)]
    return pieces, offsets


def gather_dots(state, slab, name):
    pieces, offsets = gather_rows(state)
    evens = len(offsets) - 2
    total = dots(pieces[:1], offsets[:1], (), slab, name + "_own")
    for i, (lo, hi) in enumerate(
        ((1, evens // 2), (evens // 2, evens), (evens, evens + 1), (evens + 1, evens + 2))
    ):
        if hi > lo:
            total = dots(pieces[lo:hi], offsets[lo:hi], (total,), slab, f"{name}_{i}")
    return total


def reduce_rows(step, gathered, norms, classes, targets, sigma, slab):
    rows = lax.axis_size("rows")
    slab_rows, slab_pixels = slab.shape
    span = slab_pixels // rows
    near, far = spread(rows)
    unit = 16 * slab_rows * span

    def chunks(ks, name):
        return call(
            functools.partial(chunks_kernel, ks),
            shape((len(ks), 8, span + PAD)),
            (kept, tails, in_vmem(slab)),
            flops=unit * len(ks),
            name=f"{name}_{step}",
        )

    def merged(mine, theirs, name):
        outs = [shape((8, span + PAD))] * mine.shape[0]
        return call(merge_kernel, outs, (mine, theirs), name=f"{name}_{step}")

    ks = tuple(k ^ 1 for k in far)
    across, kept, tails, aside = call(
        functools.partial(scores_kernel, step, ks),
        [
            shape((len(ks), 8, span + PAD)),
            shape((8, slab_rows)),
            shape((8, PAD)),
            shape((8, slab_rows)),
        ],
        (*gathered, norms, classes, targets, sigma, in_vmem(slab)),
        flops=unit * len(ks),
        name=f"scores_{step}",
    )
    across = exchange("rows", across, 1)
    beside = exchange("rows", chunks(tuple(k ^ 1 for k in near), "near_across"), 1)
    sent = merged(chunks(tuple(near), "near_own"), beside, "near_merge")
    parts = [exchange("rows", x, k) if k else x for x, k in zip(sent, near)]
    sent = merged(chunks(tuple(far), "far_own"), across, "far_merge")
    parts += [exchange("rows", x, k) for x, k in zip(sent, far)]
    return parts, aside


def squares_kernel(*refs):
    *pieces, out = refs
    total = jnp.zeros(out.shape, f32)
    for piece in pieces:
        span = piece.shape[-1] - PAD
        if len(piece.shape) == 2:
            total = total + piece[:, span:]
        else:
            total = total + jnp.sum(piece[:, :, span:], axis=0)
    out[...] = total


def finish_kernel(offsets, *refs):
    *pieces, squares, out = refs
    total = jnp.sum(squares[...], axis=0)[:, :1]
    scale = 1.0 / jnp.sqrt(total / IMAGE_POINTS + RMS_EPSILON)
    for piece, ks in zip(pieces, offsets):
        span = piece.shape[-1] - PAD
        for i, k in enumerate(ks):
            block = piece if len(piece.shape) == 2 else piece.at[i]
            out[:, block_at(k, span)] = block[:, :span] * scale


def exchange(axis, x, flip):
    return lax.ppermute(x, axis, [(i, i ^ flip) for i in range(lax.axis_size(axis))])


def sum_rows(x, beside=()):
    rows = lax.axis_size("rows")
    parts = [exchange("rows", x, k) for k in range(2, rows, 2)]
    done = [work(x) for work in beside]
    if done:
        parts, done[0] = lax.optimization_barrier((parts, done[0]))
    mine = sum(parts, x)
    other = exchange("rows", mine, 1)
    if done:
        other, done[1] = lax.optimization_barrier((other, done[1]))
    return jnp.stack([mine, other]), done


def to_readers(x, turn):
    rows, px = lax.axis_size("rows"), lax.axis_size("px")
    per = rows // px
    pairs = []
    for r in range(rows):
        for p in range(px):
            upper, core = divmod(p, 2)
            place = (2 * upper + core) ^ turn
            pairs.append((r * px + p, (place * per + r % per) * px + r // per))
    return lax.ppermute(x, ("rows", "px"), pairs)


def shards(
    queries, pixel_mean, eigenbasis, eigenvalues, level_ids, slab, slab_classes, target_categories
):
    rows = lax.axis_size("rows")
    pixels, comps = eigenbasis.shape
    slab_rows, slab_pixels = slab.shape
    span = slab_pixels // rows
    values = eigenvalues[None, :]
    classes = slab_classes[None, :]
    targets = target_categories[None, :]
    gauss_flops = 8 * pixels * comps

    copies, offset, *basis, sigma, mean = load_project(
        queries, pixel_mean[None, :], eigenbasis, level_ids
    )
    parts, (theirs, mine) = sum_rows(
        copies,
        [
            functools.partial(turned, basis[1], "theirs"),
            functools.partial(turned, basis[0], "mine"),
        ],
    )
    sent = exchange("px", back(0, "whole", parts, values, sigma, theirs, "theirs"), 1)
    image = back(0, "whole", parts, values, sigma, mine, "mine") + sent
    across = exchange("px", image, 2)
    norms = call(
        norms_kernel,
        shape((1, slab_rows)),
        (in_vmem(slab),),
        scratch=[pltpu.VMEM((slab_rows, 128), f32)],
        flops=2 * slab_rows * slab_pixels,
        name="norms",
    )
    across, norms = lax.optimization_barrier((across, norms))
    offset = call(
        first_update_kernel,
        shape((8, pixels // 2)),
        (image, across, offset, sigma),
        name="first_update",
    )
    other = exchange("px", offset, 1)
    own = call(
        project_kernel,
        shape((8, comps)),
        (offset, in_vmem(basis[0])),
        flops=gauss_flops,
        name="project_own",
    )
    copies = call(
        project_rest_kernel,
        shape((8, comps)),
        (other, own, in_vmem(theirs)),
        flops=gauss_flops,
        name="project_rest",
    )
    parts, _ = sum_rows(copies)
    sent = exchange("px", back(1, "whole", parts, values, sigma, theirs, "theirs"), 1)
    given = call(
        give_kernel,
        shape((8, pixels // 4)),
        (back(1, "give", parts, values, sigma, mine, "give"), sent),
        name="give",
    )
    given = exchange("px", given, 2)
    piece = call(
        second_update_kernel,
        shape((8, pixels // 4)),
        (back(1, "keep", parts, values, sigma, mine, "keep"), sent, given, offset, mean, sigma),
        name="second_update",
    )
    state, products = read_slices(piece, norms, slab)
    scale = norms
    for step in range(2):
        gathered = [products] + [exchange("px", products, k) for k in (2, 3, 1)]
        parts, aside = reduce_rows(step, gathered, norms, classes, targets, sigma, slab)
        if step == 0:
            norms = aside
        else:
            scale = aside
        state = call(
            functools.partial(combine_kernel, step, len(parts)),
            shape((8, span + PAD)),
            (*parts, state, scale, sigma),
            name=f"combine_{step}",
        )
        if step == 0:
            products = gather_dots(state, slab, "dots_1")
    pieces, offsets = gather_rows(state)
    squares = call(squares_kernel, shape((8, PAD)), pieces, name="squares")
    squares = jnp.stack([squares] + [exchange("px", squares, k) for k in (2, 3, 1)])
    return call(
        functools.partial(finish_kernel, offsets),
        shape((8, slab_pixels)),
        (*pieces, squares),
        name="finish",
    )


def solution(mesh):
    in_specs = (
        P(None, "rows"),
        P("rows"),
        P("rows", "px"),
        P("px"),
        P(),
        P("rows", "px"),
        P("rows"),
        P(),
    )
    out_specs = P(None, "px")
    return jax.shard_map(shards, mesh=mesh, in_specs=in_specs, out_specs=out_specs, check_vma=False)
```

```python
import functools
import math

import jax
import jax.numpy as jnp
from jax import lax
from jax.experimental import pallas as pl
from jax.experimental.pallas import tpu as pltpu
from jax.sharding import PartitionSpec as P

IMAGE_POINTS = 65536
LEVELS = 64
STEERING = 1.5
RMS_EPSILON = 1e-06
MIB = 1024 * 1024
NT = (((1,), (1,)), ((), ()))
CHUNKS = 16
PAD = 128

f32 = jnp.float32
bf16 = jnp.bfloat16


def vmem():
    return pl.BlockSpec(memory_space=pltpu.VMEM)


def anywhere():
    return pl.BlockSpec(memory_space=pl.ANY)


def in_vmem(x):
    return pltpu.with_memory_space_constraint(x, pltpu.VMEM)


def shape(dims, dtype=f32):
    return jax.ShapeDtypeStruct(dims, dtype)


def call(kernel, out_shape, args, in_specs=None, scratch=(), flops=0, name=None):
    many = isinstance(out_shape, (list, tuple))
    return pl.pallas_call(
        kernel,
        in_specs=in_specs or [vmem()] * len(args),
        out_specs=[vmem()] * len(out_shape) if many else vmem(),
        out_shape=out_shape,
        scratch_shapes=list(scratch),
        compiler_params=pltpu.CompilerParams(vmem_limit_bytes=4 * MIB),
        cost_estimate=pl.CostEstimate(
            flops=flops, bytes_accessed=16 * MIB if flops else MIB, transcendentals=0
        ),
        name=name,
    )(*args)


def rows_at(start, count, unit):
    return pl.ds(pl.multiple_of(start, unit), count)


def column(row):
    count = row.shape[1]
    down = lax.broadcasted_iota(jnp.int32, (count, count), 0)
    across = lax.broadcasted_iota(jnp.int32, (count, count), 1)
    return jnp.sum(jnp.where(down == across, row, 0.0), axis=1, keepdims=True)


def load_project_kernel(
    q_hbm, mean_hbm, e_hbm, levels_hbm, copies, offset, mine, theirs, sigma, mean, q, levels, sems
):
    pixels = e_hbm.shape[0]
    chunk = pixels // CHUNKS

    core = lax.rem(lax.axis_index("px"), 2)
    sides = ((core, mine), (1 - core, theirs))

    def source(side, c):
        return rows_at(side * (pixels // 2) + c * chunk, chunk, chunk)

    def move(i, c):
        side, held = sides[i]
        to = rows_at(c * chunk, chunk, chunk)
        return pltpu.make_async_copy(
            e_hbm.at[source(side, c)], held.at[to], sems.at[i * (CHUNKS // 2) + c]
        )

    small = [
        pltpu.make_async_copy(source, held, sems.at[CHUNKS + i])
        for i, (source, held) in enumerate(
            ((levels_hbm, levels), (q_hbm, q), (mean_hbm, mean))
        )
    ]
    small[1].start()
    small[2].start()
    small[0].start()

    for i in range(2):

        @pl.loop(0, CHUNKS // 2)
        def _(c, i=i):
            move(i, c).start()

    small[0].wait()
    lane = lax.broadcasted_iota(jnp.int32, sigma.shape, 1)
    table = jnp.zeros(sigma.shape, f32)
    for t in range(levels.shape[0]):
        fraction = column(levels[t : t + 1, :].astype(f32)) / (LEVELS - 1)
        table = jnp.where(lane == t, 0.6 * jnp.exp2(fraction), table)
    sigma[...] = table

    def step(i, c, total):
        side, held = sides[i]
        move(i, c).wait()
        at = source(side, c)
        off = q[:, at] - mean[:, at]
        offset[:, at] = off
        block = held[rows_at(c * chunk, chunk, chunk), :]
        return total + jnp.dot(off.astype(bf16), block, preferred_element_type=f32)

    small[1].wait()
    small[2].wait()
    total = jnp.zeros((8, e_hbm.shape[1]), f32)
    for i in range(2):
        total = lax.fori_loop(0, CHUNKS // 2, functools.partial(step, i), total)
    copies[...] = total


def load_project(queries, mean, basis, levels):
    pixels, comps = basis.shape
    queries, mean, basis, levels = [
        pltpu.with_memory_space_constraint(x, pltpu.HBM) for x in (queries, mean, basis, levels)
    ]
    return call(
        load_project_kernel,
        [
            shape((8, comps)),
            shape((8, pixels)),
            pltpu.VMEM((pixels // 2, comps), bf16),
            pltpu.VMEM((pixels // 2, comps), bf16),
            shape((8, PAD)),
            shape((1, pixels)),
        ],
        (queries, mean, basis, levels),
        in_specs=[anywhere()] * 4,
        scratch=[
            pltpu.VMEM((8, pixels), f32),
            pltpu.VMEM(levels.shape, jnp.int32),
            pltpu.SemaphoreType.DMA((CHUNKS + 3,)),
        ],
        flops=16 * pixels * comps,
        name="load_project",
    )


def turn_kernel(anchor, half, out):
    pixels = half.shape[0]
    tile = min(1024, pixels)

    @pl.loop(0, pixels // tile)
    def _(i):
        at = rows_at(i * tile, tile, tile)
        for k in range(out.shape[0] // 128):
            comps = slice(k * 128, (k + 1) * 128)
            out[comps, at] = half[at, comps].T


def turned(half, name, anchor):
    pixels, comps = half.shape
    return call(
        turn_kernel,
        pltpu.VMEM((comps, pixels), bf16),
        (anchor, in_vmem(half)),
        flops=pixels * comps,
        name=f"turn_{name}",
    )


def back_kernel(step, part, parts, eigenvalues, sigma, half, image):
    span = image.shape[1]
    now = sigma[:, step : step + 1]
    coeff = jnp.sum(parts[...], axis=0)
    ev = eigenvalues[...]
    shrunk = (coeff * (ev / (ev + now * now))).astype(bf16)
    if part == "whole":
        image[...] = jnp.dot(shrunk, half[...], preferred_element_type=f32)
    else:
        upper = lax.div(lax.axis_index("px"), 2)
        at = rows_at((upper if part == "keep" else 1 - upper) * span, span, span)
        image[...] = jnp.dot(shrunk, half[:, at], preferred_element_type=f32)


def back(step, part, parts, eigenvalues, sigma, half, name):
    comps, pixels = half.shape
    span = pixels if part == "whole" else pixels // 2
    return call(
        functools.partial(back_kernel, step, part),
        shape((8, span)),
        (parts, eigenvalues, sigma, in_vmem(half)),
        flops=16 * span * comps,
        name=f"back_{step}_{name}",
    )


def project_kernel(off, half, out):
    out[...] = jnp.dot(off[...].astype(bf16), half[...], preferred_element_type=f32)


def project_rest_kernel(off, own, half, out):
    part = lax.dot_general(off[...].astype(bf16), half[...], NT, preferred_element_type=f32)
    out[...] = own[...] + part


def first_update_kernel(mine, theirs, offset, sigma, out):
    half = mine.shape[1]
    core = lax.rem(lax.axis_index("px"), 2)
    ratio = sigma[:, 1:2] / sigma[:, 0:1]
    image = mine[...] + theirs[...]
    out[...] = image + ratio * (offset[:, rows_at(core * half, half, half)] - image)


def give_kernel(image, other, out):
    span = image.shape[1]
    upper = lax.div(lax.axis_index("px"), 2)
    out[...] = image[...] + other[:, rows_at((1 - upper) * span, span, span)]


def second_update_kernel(image, other, given, offset, mean, sigma, out):
    span = image.shape[1]
    place = lax.axis_index("px")
    core, upper = lax.rem(place, 2), lax.div(place, 2)
    ratio = sigma[:, 2:3] / sigma[:, 1:2]
    at = rows_at(upper * span, span, span)
    total = image[...] + other[:, at] + given[...]
    average = mean[:, rows_at((2 * core + upper) * span, span, span)]
    out[...] = average + total + ratio * (offset[:, at] - total)


def norms_kernel(slab, out, folded):
    rows, pixels = slab.shape
    height, tile = 64, 512

    @pl.loop(0, rows // height)
    def _(b):
        at = rows_at(b * height, height, height)

        def step(i, total):
            part = slab[at, rows_at(i * tile, tile, tile)].astype(f32)
            for k in range(tile // 128):
                piece = part[:, k * 128 : (k + 1) * 128]
                total = total + piece * piece
            return total

        folded[at, :] = lax.fori_loop(0, pixels // tile, step, jnp.zeros((height, 128), f32))

    out[...] = jnp.sum(folded[...], axis=1)[None, :]


def block_at(k, span):
    px = lax.axis_size("px")
    per = lax.axis_size("rows") // px
    other = lax.bitwise_xor(lax.axis_index("rows"), k)
    place = lax.div(other, per)
    place = lax.rem(place, 2) * (px // 2) + lax.div(place, 2)
    return rows_at((lax.rem(other, per) * px + place) * span, span, span)


def dots_kernel(offsets, fresh, *refs):
    *inputs, slab, out = refs
    pieces, before = inputs[: len(offsets)], inputs[len(offsets) :]
    span = slab.shape[1] // lax.axis_size("rows")
    total = before[0][:8] if before and not fresh else jnp.zeros((8, slab.shape[0]), f32)
    rest = before[0][8:] if before else jnp.zeros((8, slab.shape[0]), f32)
    for piece, ks in zip(pieces, offsets):
        for i, k in enumerate(ks):
            block = piece if len(piece.shape) == 2 else piece.at[i]
            total = total + lax.dot_general(
                block[:, :span].astype(bf16),
                slab[:, block_at(k, span)],
                NT,
                preferred_element_type=f32,
            )
            if block.shape[1] > span:
                lane = lax.broadcasted_iota(jnp.int32, rest.shape, 1)
                rest = rest + jnp.where(lane >= 0, block[:, span : span + 1], 0.0)
    out[:8] = total
    out[8:] = rest


def dots(pieces, offsets, before, slab, name, fresh=False):
    rows = lax.axis_size("rows")
    count = sum(len(ks) for ks in offsets)
    return call(
        functools.partial(dots_kernel, offsets, fresh),
        shape((16, slab.shape[0])),
        (*pieces, *before, in_vmem(slab)),
        flops=16 * count * slab.shape[0] * (slab.shape[1] // rows),
        name=name,
    )


def read_slices(piece, norms, slab):
    rows, px = lax.axis_size("rows"), lax.axis_size("px")
    per = rows // px
    got = [to_readers(piece, turn) for turn in range(px)]
    halves = [range(1, px, 2), range(0, px, 2)]
    packs = [jnp.stack([got[t] for t in half]) for half in halves]
    groups = [([got[t] for t in half], [(t * per,) for t in half]) for half in halves]
    for k in range(1, per):
        for pack, half in zip(packs, halves):
            groups.append(([exchange("rows", pack, k)], [tuple(t * per ^ k for t in half)]))
    total = (jnp.broadcast_to(norms, (16, slab.shape[0])),)
    for i, (pieces, offsets) in enumerate(groups):
        total = (dots(pieces, offsets, total, slab, f"dots_0_{i}", i == 0),)
    return got[0], total[0]


def put_chunks(weights, tail, ks, slab, out):
    span = slab.shape[1] // lax.axis_size("rows")
    for i, k in enumerate(ks):
        out[i, :, :span] = jnp.dot(
            weights, slab[:, block_at(k, span)], preferred_element_type=f32
        )
        out[i, :, span:] = tail


def scores_kernel(step, ks, g0, g1, g2, g3, norms, classes, targets, sigma, slab, out, kept, tails, aside):
    both = (g0[...] + g1[...]) + (g2[...] + g3[...])
    inner = both[:8]
    if step == 0:
        norm = both[8:9]
        aside[...] = jnp.broadcast_to(norm, aside.shape)
    else:
        norm = norms[:1]
        scale = jnp.sqrt(both[8:, :1] / IMAGE_POINTS + RMS_EPSILON)
        inner = inner / scale
        aside[...] = jnp.broadcast_to(scale, aside.shape)
    now = sigma[:, 2 + step : 3 + step]
    sharp = 1.0 / (2.0 * now * now * math.sqrt(IMAGE_POINTS))
    wanted = column(targets[...].astype(f32))
    bonus = jnp.where(classes[...].astype(f32) == wanted, STEERING, 0.0).astype(f32)
    scores = sharp * (2.0 * inner - norm) + bonus
    peak = jnp.max(scores, axis=1, keepdims=True)
    weights = jnp.exp(scores - peak).astype(bf16)
    kept[...] = weights.astype(f32)
    mass = jnp.sum(weights.astype(f32), axis=1, keepdims=True)
    lane = lax.broadcasted_iota(jnp.int32, (8, PAD), 1)
    tail = jnp.where(lane < PAD // 2, peak, mass)
    tails[...] = tail
    put_chunks(weights, tail, ks, slab, out)


def chunks_kernel(ks, kept, tails, slab, out):
    put_chunks(kept[...].astype(bf16), tails[...], ks, slab, out)


def merge(parts, span):
    peaks = [part[:, span : span + 1] for part in parts]
    masses = [part[:, span + PAD // 2 : span + PAD // 2 + 1] for part in parts]
    top = functools.reduce(jnp.maximum, peaks)
    total, mass = 0.0, 0.0
    for part, peak, part_mass in zip(parts, peaks, masses):
        factor = jnp.exp(peak - top)
        total = total + factor * part[:, :span]
        mass = mass + factor * part_mass
    return top, mass, total


def merge_kernel(mine, theirs, *outs):
    span = mine.shape[2] - PAD
    lane = lax.broadcasted_iota(jnp.int32, (8, PAD), 1)
    for i, out in enumerate(outs):
        top, mass, total = merge([mine.at[i], theirs.at[i]], span)
        out[:, :span] = total
        out[:, span:] = jnp.where(lane < PAD // 2, top, mass)


def combine_kernel(step, count, *refs):
    parts = refs[:count]
    state, scale, sigma, out = refs[count:]
    span = out.shape[1] - PAD
    _, mass, total = merge(parts, span)
    average = total / mass
    ratio = sigma[:, 3 + step : 4 + step] / sigma[:, 2 + step : 3 + step]
    current = state[:, :span]
    if step:
        current = current / scale[:, :1]
    update = average + ratio * (current - average)
    out[:, :span] = update
    out[:, span:] = jnp.broadcast_to(jnp.sum(update * update, axis=1, keepdims=True), (8, PAD))


def spread(flat):
    evens = list(range(0, flat, 2))
    near, far = evens[: len(evens) // 2], evens[len(evens) // 2 :]
    return near, far


def gather_rows(state):
    rows = lax.axis_size("rows")
    near, far = spread(rows)
    got = {k: exchange("rows", state, k) if k else state for k in near + far}
    one, two = near[:1] + far[:-1], near[1:] + far[-1:]
    first = exchange("rows", jnp.stack([got[k] for k in one]), 1)
    second = exchange("rows", jnp.stack([got[k] for k in two]), 1)
    pieces = [got[k] for k in near + far] + [first, second]
    offsets = [(k,) for k in near + far]
    offsets += [tuple(k ^ 1 for k in one), tuple(k ^ 1 for k in two)]
    return pieces, offsets


def gather_dots(state, slab, name):
    pieces, offsets = gather_rows(state)
    evens = len(offsets) - 2
    total = dots(pieces[:1], offsets[:1], (), slab, name + "_own")
    for i, (lo, hi) in enumerate(
        ((1, evens // 2), (evens // 2, evens), (evens, evens + 1), (evens + 1, evens + 2))
    ):
        if hi > lo:
            total = dots(pieces[lo:hi], offsets[lo:hi], (total,), slab, f"{name}_{i}")
    return total


def reduce_rows(step, gathered, norms, classes, targets, sigma, slab):
    rows = lax.axis_size("rows")
    slab_rows, slab_pixels = slab.shape
    span = slab_pixels // rows
    near, far = spread(rows)
    unit = 16 * slab_rows * span

    def chunks(ks, name):
        return call(
            functools.partial(chunks_kernel, ks),
            shape((len(ks), 8, span + PAD)),
            (kept, tails, in_vmem(slab)),
            flops=unit * len(ks),
            name=f"{name}_{step}",
        )

    def merged(mine, theirs, name):
        outs = [shape((8, span + PAD))] * mine.shape[0]
        return call(merge_kernel, outs, (mine, theirs), name=f"{name}_{step}")

    ks = tuple(k ^ 1 for k in far)
    across, kept, tails, aside = call(
        functools.partial(scores_kernel, step, ks),
        [
            shape((len(ks), 8, span + PAD)),
            shape((8, slab_rows)),
            shape((8, PAD)),
            shape((8, slab_rows)),
        ],
        (*gathered, norms, classes, targets, sigma, in_vmem(slab)),
        flops=unit * len(ks),
        name=f"scores_{step}",
    )
    across = exchange("rows", across, 1)
    beside = exchange("rows", chunks(tuple(k ^ 1 for k in near), "near_across"), 1)
    sent = merged(chunks(tuple(near), "near_own"), beside, "near_merge")
    parts = [exchange("rows", x, k) if k else x for x, k in zip(sent, near)]
    sent = merged(chunks(tuple(far), "far_own"), across, "far_merge")
    parts += [exchange("rows", x, k) for x, k in zip(sent, far)]
    return parts, aside


def squares_kernel(*refs):
    *pieces, out = refs
    total = jnp.zeros(out.shape, f32)
    for piece in pieces:
        span = piece.shape[-1] - PAD
        if len(piece.shape) == 2:
            total = total + piece[:, span:]
        else:
            total = total + jnp.sum(piece[:, :, span:], axis=0)
    out[...] = total


def finish_kernel(offsets, *refs):
    *pieces, squares, out = refs
    total = jnp.sum(squares[...], axis=0)[:, :1]
    scale = 1.0 / jnp.sqrt(total / IMAGE_POINTS + RMS_EPSILON)
    for piece, ks in zip(pieces, offsets):
        span = piece.shape[-1] - PAD
        for i, k in enumerate(ks):
            block = piece if len(piece.shape) == 2 else piece.at[i]
            out[:, block_at(k, span)] = block[:, :span] * scale


def exchange(axis, x, flip):
    return lax.ppermute(x, axis, [(i, i ^ flip) for i in range(lax.axis_size(axis))])


def sum_rows(x, beside=()):
    rows = lax.axis_size("rows")
    parts = [exchange("rows", x, k) for k in range(rows - 2, 0, -2)]
    done = [work(x) for work in beside]
    if done:
        parts, done[0] = lax.optimization_barrier((parts, done[0]))
    mine = sum(parts, x)
    other = exchange("rows", mine, 1)
    if done:
        other, done[1] = lax.optimization_barrier((other, done[1]))
    return jnp.stack([mine, other]), done


def to_readers(x, turn):
    rows, px = lax.axis_size("rows"), lax.axis_size("px")
    per = rows // px
    pairs = []
    for r in range(rows):
        for p in range(px):
            upper, core = divmod(p, 2)
            place = (2 * upper + core) ^ turn
            pairs.append((r * px + p, (place * per + r % per) * px + r // per))
    return lax.ppermute(x, ("rows", "px"), pairs)


def shards(
    queries, pixel_mean, eigenbasis, eigenvalues, level_ids, slab, slab_classes, target_categories
):
    rows = lax.axis_size("rows")
    pixels, comps = eigenbasis.shape
    slab_rows, slab_pixels = slab.shape
    span = slab_pixels // rows
    values = eigenvalues[None, :]
    classes = slab_classes[None, :]
    targets = target_categories[None, :]
    gauss_flops = 8 * pixels * comps

    copies, offset, *basis, sigma, mean = load_project(
        queries, pixel_mean[None, :], eigenbasis, level_ids
    )
    parts, (theirs, mine) = sum_rows(
        copies,
        [
            functools.partial(turned, basis[1], "theirs"),
            functools.partial(turned, basis[0], "mine"),
        ],
    )
    sent = exchange("px", back(0, "whole", parts, values, sigma, theirs, "theirs"), 1)
    image = back(0, "whole", parts, values, sigma, mine, "mine") + sent
    across = exchange("px", image, 2)
    norms = call(
        norms_kernel,
        shape((1, slab_rows)),
        (in_vmem(slab),),
        scratch=[pltpu.VMEM((slab_rows, 128), f32)],
        flops=2 * slab_rows * slab_pixels,
        name="norms",
    )
    across, norms = lax.optimization_barrier((across, norms))
    offset = call(
        first_update_kernel,
        shape((8, pixels // 2)),
        (image, across, offset, sigma),
        name="first_update",
    )
    other = exchange("px", offset, 1)
    own = call(
        project_kernel,
        shape((8, comps)),
        (offset, in_vmem(basis[0])),
        flops=gauss_flops,
        name="project_own",
    )
    copies = call(
        project_rest_kernel,
        shape((8, comps)),
        (other, own, in_vmem(theirs)),
        flops=gauss_flops,
        name="project_rest",
    )
    parts, _ = sum_rows(copies)
    sent = exchange("px", back(1, "whole", parts, values, sigma, theirs, "theirs"), 1)
    given = call(
        give_kernel,
        shape((8, pixels // 4)),
        (back(1, "give", parts, values, sigma, mine, "give"), sent),
        name="give",
    )
    given = exchange("px", given, 2)
    piece = call(
        second_update_kernel,
        shape((8, pixels // 4)),
        (back(1, "keep", parts, values, sigma, mine, "keep"), sent, given, offset, mean, sigma),
        name="second_update",
    )
    state, products = read_slices(piece, norms, slab)
    scale = norms
    for step in range(2):
        gathered = [products] + [exchange("px", products, k) for k in (2, 3, 1)]
        parts, aside = reduce_rows(step, gathered, norms, classes, targets, sigma, slab)
        if step == 0:
            norms = aside
        else:
            scale = aside
        state = call(
            functools.partial(combine_kernel, step, len(parts)),
            shape((8, span + PAD)),
            (*parts, state, scale, sigma),
            name=f"combine_{step}",
        )
        if step == 0:
            products = gather_dots(state, slab, "dots_1")
    pieces, offsets = gather_rows(state)
    squares = call(squares_kernel, shape((8, PAD)), pieces, name="squares")
    squares = jnp.stack([squares] + [exchange("px", squares, k) for k in (2, 3, 1)])
    return call(
        functools.partial(finish_kernel, offsets),
        shape((8, slab_pixels)),
        (*pieces, squares),
        name="finish",
    )


def solution(mesh):
    in_specs = (
        P(None, "rows"),
        P("rows"),
        P("rows", "px"),
        P("px"),
        P(),
        P("rows", "px"),
        P("rows"),
        P(),
    )
    out_specs = P(None, "px")
    return jax.shard_map(shards, mesh=mesh, in_specs=in_specs, out_specs=out_specs, check_vma=False)
```

```python
import functools
import math

import jax
import jax.numpy as jnp
from jax import lax
from jax.experimental import pallas as pl
from jax.experimental.pallas import tpu as pltpu
from jax.sharding import PartitionSpec as P

IMAGE_POINTS = 65536
LEVELS = 64
STEERING = 1.5
RMS_EPSILON = 1e-06
MIB = 1024 * 1024
NT = (((1,), (1,)), ((), ()))
CHUNKS = 16
PAD = 128

f32 = jnp.float32
bf16 = jnp.bfloat16


def vmem():
    return pl.BlockSpec(memory_space=pltpu.VMEM)


def anywhere():
    return pl.BlockSpec(memory_space=pl.ANY)


def in_vmem(x):
    return pltpu.with_memory_space_constraint(x, pltpu.VMEM)


def shape(dims, dtype=f32):
    return jax.ShapeDtypeStruct(dims, dtype)


def call(kernel, out_shape, args, in_specs=None, scratch=(), flops=0, name=None):
    many = isinstance(out_shape, (list, tuple))
    return pl.pallas_call(
        kernel,
        in_specs=in_specs or [vmem()] * len(args),
        out_specs=[vmem()] * len(out_shape) if many else vmem(),
        out_shape=out_shape,
        scratch_shapes=list(scratch),
        compiler_params=pltpu.CompilerParams(vmem_limit_bytes=4 * MIB),
        cost_estimate=pl.CostEstimate(
            flops=flops, bytes_accessed=16 * MIB if flops else MIB, transcendentals=0
        ),
        name=name,
    )(*args)


def rows_at(start, count, unit):
    return pl.ds(pl.multiple_of(start, unit), count)


def column(row):
    count = row.shape[1]
    down = lax.broadcasted_iota(jnp.int32, (count, count), 0)
    across = lax.broadcasted_iota(jnp.int32, (count, count), 1)
    return jnp.sum(jnp.where(down == across, row, 0.0), axis=1, keepdims=True)


def load_project_kernel(
    q_hbm, mean_hbm, e_hbm, levels_hbm, copies, offset, mine, theirs, sigma, mean, q, levels, sems
):
    pixels = e_hbm.shape[0]
    chunk = pixels // CHUNKS

    core = lax.rem(lax.axis_index("px"), 2)
    sides = ((core, mine), (1 - core, theirs))

    def source(side, c):
        return rows_at(side * (pixels // 2) + c * chunk, chunk, chunk)

    def move(i, c):
        side, held = sides[i]
        to = rows_at(c * chunk, chunk, chunk)
        return pltpu.make_async_copy(
            e_hbm.at[source(side, c)], held.at[to], sems.at[i * (CHUNKS // 2) + c]
        )

    small = [
        pltpu.make_async_copy(source, held, sems.at[CHUNKS + i])
        for i, (source, held) in enumerate(
            ((levels_hbm, levels), (q_hbm, q), (mean_hbm, mean))
        )
    ]
    small[1].start()
    small[2].start()
    small[0].start()

    for i in range(2):

        @pl.loop(0, CHUNKS // 2)
        def _(c, i=i):
            move(i, c).start()

    small[0].wait()
    lane = lax.broadcasted_iota(jnp.int32, sigma.shape, 1)
    table = jnp.zeros(sigma.shape, f32)
    for t in range(levels.shape[0]):
        fraction = column(levels[t : t + 1, :].astype(f32)) / (LEVELS - 1)
        table = jnp.where(lane == t, 0.6 * jnp.exp2(fraction), table)
    sigma[...] = table

    def step(i, c, total):
        side, held = sides[i]
        move(i, c).wait()
        at = source(side, c)
        off = q[:, at] - mean[:, at]
        offset[:, at] = off
        block = held[rows_at(c * chunk, chunk, chunk), :]
        return total + jnp.dot(off.astype(bf16), block, preferred_element_type=f32)

    small[1].wait()
    small[2].wait()
    total = jnp.zeros((8, e_hbm.shape[1]), f32)
    for i in range(2):
        total = lax.fori_loop(0, CHUNKS // 2, functools.partial(step, i), total)
    copies[...] = total


def load_project(queries, mean, basis, levels):
    pixels, comps = basis.shape
    queries, mean, basis, levels = [
        pltpu.with_memory_space_constraint(x, pltpu.HBM) for x in (queries, mean, basis, levels)
    ]
    return call(
        load_project_kernel,
        [
            shape((8, comps)),
            shape((8, pixels)),
            pltpu.VMEM((pixels // 2, comps), bf16),
            pltpu.VMEM((pixels // 2, comps), bf16),
            shape((8, PAD)),
            shape((1, pixels)),
        ],
        (queries, mean, basis, levels),
        in_specs=[anywhere()] * 4,
        scratch=[
            pltpu.VMEM((8, pixels), f32),
            pltpu.VMEM(levels.shape, jnp.int32),
            pltpu.SemaphoreType.DMA((CHUNKS + 3,)),
        ],
        flops=16 * pixels * comps,
        name="load_project",
    )


def turn_kernel(anchor, half, out):
    pixels = half.shape[0]
    tile = min(1024, pixels)

    @pl.loop(0, pixels // tile)
    def _(i):
        at = rows_at(i * tile, tile, tile)
        for k in range(out.shape[0] // 128):
            comps = slice(k * 128, (k + 1) * 128)
            out[comps, at] = half[at, comps].T


def turned(half, name, anchor):
    pixels, comps = half.shape
    return call(
        turn_kernel,
        pltpu.VMEM((comps, pixels), bf16),
        (anchor, in_vmem(half)),
        flops=pixels * comps,
        name=f"turn_{name}",
    )


def back_kernel(step, part, parts, eigenvalues, sigma, half, image):
    span = image.shape[1]
    now = sigma[:, step : step + 1]
    coeff = jnp.sum(parts[...], axis=0)
    ev = eigenvalues[...]
    shrunk = (coeff * (ev / (ev + now * now))).astype(bf16)
    if part == "whole":
        image[...] = jnp.dot(shrunk, half[...], preferred_element_type=f32)
    else:
        upper = lax.div(lax.axis_index("px"), 2)
        at = rows_at((upper if part == "keep" else 1 - upper) * span, span, span)
        image[...] = jnp.dot(shrunk, half[:, at], preferred_element_type=f32)


def back(step, part, parts, eigenvalues, sigma, half, name):
    comps, pixels = half.shape
    span = pixels if part == "whole" else pixels // 2
    return call(
        functools.partial(back_kernel, step, part),
        shape((8, span)),
        (parts, eigenvalues, sigma, in_vmem(half)),
        flops=16 * span * comps,
        name=f"back_{step}_{name}",
    )


def project_kernel(off, half, out):
    out[...] = jnp.dot(off[...].astype(bf16), half[...], preferred_element_type=f32)


def project_rest_kernel(off, own, half, out):
    part = lax.dot_general(off[...].astype(bf16), half[...], NT, preferred_element_type=f32)
    out[...] = own[...] + part


def first_update_kernel(mine, theirs, offset, sigma, out):
    half = mine.shape[1]
    core = lax.rem(lax.axis_index("px"), 2)
    ratio = sigma[:, 1:2] / sigma[:, 0:1]
    image = mine[...] + theirs[...]
    out[...] = image + ratio * (offset[:, rows_at(core * half, half, half)] - image)


def give_kernel(image, other, out):
    span = image.shape[1]
    upper = lax.div(lax.axis_index("px"), 2)
    out[...] = image[...] + other[:, rows_at((1 - upper) * span, span, span)]


def second_update_kernel(image, other, given, offset, mean, sigma, out):
    span = image.shape[1]
    place = lax.axis_index("px")
    core, upper = lax.rem(place, 2), lax.div(place, 2)
    ratio = sigma[:, 2:3] / sigma[:, 1:2]
    at = rows_at(upper * span, span, span)
    total = image[...] + other[:, at] + given[...]
    average = mean[:, rows_at((2 * core + upper) * span, span, span)]
    out[...] = average + total + ratio * (offset[:, at] - total)


def norms_kernel(slab, out, folded):
    rows, pixels = slab.shape
    height, tile = 64, 512

    @pl.loop(0, rows // height)
    def _(b):
        at = rows_at(b * height, height, height)

        def step(i, total):
            part = slab[at, rows_at(i * tile, tile, tile)].astype(f32)
            for k in range(tile // 128):
                piece = part[:, k * 128 : (k + 1) * 128]
                total = total + piece * piece
            return total

        folded[at, :] = lax.fori_loop(0, pixels // tile, step, jnp.zeros((height, 128), f32))

    out[...] = jnp.sum(folded[...], axis=1)[None, :]


def block_at(k, span):
    px = lax.axis_size("px")
    per = lax.axis_size("rows") // px
    other = lax.bitwise_xor(lax.axis_index("rows"), k)
    place = lax.div(other, per)
    place = lax.rem(place, 2) * (px // 2) + lax.div(place, 2)
    return rows_at((lax.rem(other, per) * px + place) * span, span, span)


def dots_kernel(offsets, fresh, *refs):
    *inputs, slab, out = refs
    pieces, before = inputs[: len(offsets)], inputs[len(offsets) :]
    span = slab.shape[1] // lax.axis_size("rows")
    total = before[0][:8] if before and not fresh else jnp.zeros((8, slab.shape[0]), f32)
    rest = before[0][8:] if before else jnp.zeros((8, slab.shape[0]), f32)
    for piece, ks in zip(pieces, offsets):
        for i, k in enumerate(ks):
            block = piece if len(piece.shape) == 2 else piece.at[i]
            total = total + lax.dot_general(
                block[:, :span].astype(bf16),
                slab[:, block_at(k, span)],
                NT,
                preferred_element_type=f32,
            )
            if block.shape[1] > span:
                lane = lax.broadcasted_iota(jnp.int32, rest.shape, 1)
                rest = rest + jnp.where(lane >= 0, block[:, span : span + 1], 0.0)
    out[:8] = total
    out[8:] = rest


def dots(pieces, offsets, before, slab, name, fresh=False):
    rows = lax.axis_size("rows")
    count = sum(len(ks) for ks in offsets)
    return call(
        functools.partial(dots_kernel, offsets, fresh),
        shape((16, slab.shape[0])),
        (*pieces, *before, in_vmem(slab)),
        flops=16 * count * slab.shape[0] * (slab.shape[1] // rows),
        name=name,
    )


def read_slices(piece, norms, slab):
    rows, px = lax.axis_size("rows"), lax.axis_size("px")
    per = rows // px
    got = [to_readers(piece, turn) for turn in range(px)]
    halves = [range(1, px - 1), [0, px - 1]]
    packs = [jnp.stack([got[t] for t in half]) for half in halves]
    groups = [([got[t] for t in half], [(t * per,) for t in half]) for half in halves]
    for k in range(1, per):
        for pack, half in zip(packs, halves):
            groups.append(([exchange("rows", pack, k)], [tuple(t * per ^ k for t in half)]))
    total = (jnp.broadcast_to(norms, (16, slab.shape[0])),)
    for i, (pieces, offsets) in enumerate(groups):
        total = (dots(pieces, offsets, total, slab, f"dots_0_{i}", i == 0),)
    return got[0], total[0]


def put_chunks(weights, tail, ks, slab, out):
    span = slab.shape[1] // lax.axis_size("rows")
    for i, k in enumerate(ks):
        out[i, :, :span] = jnp.dot(
            weights, slab[:, block_at(k, span)], preferred_element_type=f32
        )
        out[i, :, span:] = tail


def scores_kernel(step, ks, g0, g1, g2, g3, norms, classes, targets, sigma, slab, out, kept, tails, aside):
    both = (g0[...] + g1[...]) + (g2[...] + g3[...])
    inner = both[:8]
    if step == 0:
        norm = both[8:9]
        aside[...] = jnp.broadcast_to(norm, aside.shape)
    else:
        norm = norms[:1]
        scale = jnp.sqrt(both[8:, :1] / IMAGE_POINTS + RMS_EPSILON)
        inner = inner / scale
        aside[...] = jnp.broadcast_to(scale, aside.shape)
    now = sigma[:, 2 + step : 3 + step]
    sharp = 1.0 / (2.0 * now * now * math.sqrt(IMAGE_POINTS))
    wanted = column(targets[...].astype(f32))
    bonus = jnp.where(classes[...].astype(f32) == wanted, STEERING, 0.0).astype(f32)
    scores = sharp * (2.0 * inner - norm) + bonus
    peak = jnp.max(scores, axis=1, keepdims=True)
    weights = jnp.exp(scores - peak).astype(bf16)
    kept[...] = weights.astype(f32)
    mass = jnp.sum(weights.astype(f32), axis=1, keepdims=True)
    lane = lax.broadcasted_iota(jnp.int32, (8, PAD), 1)
    tail = jnp.where(lane < PAD // 2, peak, mass)
    tails[...] = tail
    put_chunks(weights, tail, ks, slab, out)


def chunks_kernel(ks, kept, tails, slab, out):
    put_chunks(kept[...].astype(bf16), tails[...], ks, slab, out)


def merge(parts, span):
    peaks = [part[:, span : span + 1] for part in parts]
    masses = [part[:, span + PAD // 2 : span + PAD // 2 + 1] for part in parts]
    top = functools.reduce(jnp.maximum, peaks)
    total, mass = 0.0, 0.0
    for part, peak, part_mass in zip(parts, peaks, masses):
        factor = jnp.exp(peak - top)
        total = total + factor * part[:, :span]
        mass = mass + factor * part_mass
    return top, mass, total


def merge_kernel(mine, theirs, *outs):
    span = mine.shape[2] - PAD
    lane = lax.broadcasted_iota(jnp.int32, (8, PAD), 1)
    for i, out in enumerate(outs):
        top, mass, total = merge([mine.at[i], theirs.at[i]], span)
        out[:, :span] = total
        out[:, span:] = jnp.where(lane < PAD // 2, top, mass)


def combine_kernel(step, count, *refs):
    parts = refs[:count]
    state, scale, sigma, out = refs[count:]
    span = out.shape[1] - PAD
    _, mass, total = merge(parts, span)
    average = total / mass
    ratio = sigma[:, 3 + step : 4 + step] / sigma[:, 2 + step : 3 + step]
    current = state[:, :span]
    if step:
        current = current / scale[:, :1]
    update = average + ratio * (current - average)
    out[:, :span] = update
    out[:, span:] = jnp.broadcast_to(jnp.sum(update * update, axis=1, keepdims=True), (8, PAD))


def spread(flat):
    evens = list(range(0, flat, 2))
    near, far = evens[: len(evens) // 2], evens[len(evens) // 2 :]
    return near, far


def gather_rows(state):
    rows = lax.axis_size("rows")
    near, far = spread(rows)
    got = {k: exchange("rows", state, k) if k else state for k in near + far}
    one, two = near[:1] + far[:-1], near[1:] + far[-1:]
    first = exchange("rows", jnp.stack([got[k] for k in one]), 1)
    second = exchange("rows", jnp.stack([got[k] for k in two]), 1)
    pieces = [got[k] for k in near + far] + [first, second]
    offsets = [(k,) for k in near + far]
    offsets += [tuple(k ^ 1 for k in one), tuple(k ^ 1 for k in two)]
    return pieces, offsets


def gather_dots(state, slab, name):
    pieces, offsets = gather_rows(state)
    evens = len(offsets) - 2
    total = dots(pieces[:1], offsets[:1], (), slab, name + "_own")
    for i, (lo, hi) in enumerate(
        ((1, evens // 2), (evens // 2, evens), (evens, evens + 1), (evens + 1, evens + 2))
    ):
        if hi > lo:
            total = dots(pieces[lo:hi], offsets[lo:hi], (total,), slab, f"{name}_{i}")
    return total


def reduce_rows(step, gathered, norms, classes, targets, sigma, slab):
    rows = lax.axis_size("rows")
    slab_rows, slab_pixels = slab.shape
    span = slab_pixels // rows
    near, far = spread(rows)
    unit = 16 * slab_rows * span

    def chunks(ks, name):
        return call(
            functools.partial(chunks_kernel, ks),
            shape((len(ks), 8, span + PAD)),
            (kept, tails, in_vmem(slab)),
            flops=unit * len(ks),
            name=f"{name}_{step}",
        )

    def merged(mine, theirs, name):
        outs = [shape((8, span + PAD))] * mine.shape[0]
        return call(merge_kernel, outs, (mine, theirs), name=f"{name}_{step}")

    ks = tuple(k ^ 1 for k in far)
    across, kept, tails, aside = call(
        functools.partial(scores_kernel, step, ks),
        [
            shape((len(ks), 8, span + PAD)),
            shape((8, slab_rows)),
            shape((8, PAD)),
            shape((8, slab_rows)),
        ],
        (*gathered, norms, classes, targets, sigma, in_vmem(slab)),
        flops=unit * len(ks),
        name=f"scores_{step}",
    )
    across = exchange("rows", across, 1)
    beside = exchange("rows", chunks(tuple(k ^ 1 for k in near), "near_across"), 1)
    sent = merged(chunks(tuple(near), "near_own"), beside, "near_merge")
    parts = [exchange("rows", x, k) if k else x for x, k in zip(sent, near)]
    sent = merged(chunks(tuple(far), "far_own"), across, "far_merge")
    parts += [exchange("rows", x, k) for x, k in zip(sent, far)]
    return parts, aside


def squares_kernel(*refs):
    *pieces, out = refs
    total = jnp.zeros(out.shape, f32)
    for piece in pieces:
        span = piece.shape[-1] - PAD
        if len(piece.shape) == 2:
            total = total + piece[:, span:]
        else:
            total = total + jnp.sum(piece[:, :, span:], axis=0)
    out[...] = total


def finish_kernel(offsets, *refs):
    *pieces, squares, out = refs
    total = jnp.sum(squares[...], axis=0)[:, :1]
    scale = 1.0 / jnp.sqrt(total / IMAGE_POINTS + RMS_EPSILON)
    for piece, ks in zip(pieces, offsets):
        span = piece.shape[-1] - PAD
        for i, k in enumerate(ks):
            block = piece if len(piece.shape) == 2 else piece.at[i]
            out[:, block_at(k, span)] = block[:, :span] * scale


def exchange(axis, x, flip):
    return lax.ppermute(x, axis, [(i, i ^ flip) for i in range(lax.axis_size(axis))])


def sum_rows(x, beside=()):
    rows = lax.axis_size("rows")
    parts = [exchange("rows", x, k) for k in range(rows - 2, 0, -2)]
    done = [work(x) for work in beside]
    if done:
        parts, done[0] = lax.optimization_barrier((parts, done[0]))
    mine = sum(parts, x)
    other = exchange("rows", mine, 1)
    if done:
        other, done[1] = lax.optimization_barrier((other, done[1]))
    return jnp.stack([mine, other]), done


def to_readers(x, turn):
    rows, px = lax.axis_size("rows"), lax.axis_size("px")
    per = rows // px
    pairs = []
    for r in range(rows):
        for p in range(px):
            upper, core = divmod(p, 2)
            place = (2 * upper + core) ^ turn
            pairs.append((r * px + p, (place * per + r % per) * px + r // per))
    return lax.ppermute(x, ("rows", "px"), pairs)


def shards(
    queries, pixel_mean, eigenbasis, eigenvalues, level_ids, slab, slab_classes, target_categories
):
    rows = lax.axis_size("rows")
    pixels, comps = eigenbasis.shape
    slab_rows, slab_pixels = slab.shape
    span = slab_pixels // rows
    values = eigenvalues[None, :]
    classes = slab_classes[None, :]
    targets = target_categories[None, :]
    gauss_flops = 8 * pixels * comps

    copies, offset, *basis, sigma, mean = load_project(
        queries, pixel_mean[None, :], eigenbasis, level_ids
    )
    parts, (theirs, mine) = sum_rows(
        copies,
        [
            functools.partial(turned, basis[1], "theirs"),
            functools.partial(turned, basis[0], "mine"),
        ],
    )
    sent = exchange("px", back(0, "whole", parts, values, sigma, theirs, "theirs"), 1)
    image = back(0, "whole", parts, values, sigma, mine, "mine") + sent
    across = exchange("px", image, 2)
    norms = call(
        norms_kernel,
        shape((1, slab_rows)),
        (in_vmem(slab),),
        scratch=[pltpu.VMEM((slab_rows, 128), f32)],
        flops=2 * slab_rows * slab_pixels,
        name="norms",
    )
    across, norms = lax.optimization_barrier((across, norms))
    offset = call(
        first_update_kernel,
        shape((8, pixels // 2)),
        (image, across, offset, sigma),
        name="first_update",
    )
    other = exchange("px", offset, 1)
    own = call(
        project_kernel,
        shape((8, comps)),
        (offset, in_vmem(basis[0])),
        flops=gauss_flops,
        name="project_own",
    )
    copies = call(
        project_rest_kernel,
        shape((8, comps)),
        (other, own, in_vmem(theirs)),
        flops=gauss_flops,
        name="project_rest",
    )
    parts, _ = sum_rows(copies)
    sent = exchange("px", back(1, "whole", parts, values, sigma, theirs, "theirs"), 1)
    given = call(
        give_kernel,
        shape((8, pixels // 4)),
        (back(1, "give", parts, values, sigma, mine, "give"), sent),
        name="give",
    )
    given = exchange("px", given, 2)
    piece = call(
        second_update_kernel,
        shape((8, pixels // 4)),
        (back(1, "keep", parts, values, sigma, mine, "keep"), sent, given, offset, mean, sigma),
        name="second_update",
    )
    state, products = read_slices(piece, norms, slab)
    scale = norms
    for step in range(2):
        gathered = [products] + [exchange("px", products, k) for k in (2, 3, 1)]
        parts, aside = reduce_rows(step, gathered, norms, classes, targets, sigma, slab)
        if step == 0:
            norms = aside
        else:
            scale = aside
        state = call(
            functools.partial(combine_kernel, step, len(parts)),
            shape((8, span + PAD)),
            (*parts, state, scale, sigma),
            name=f"combine_{step}",
        )
        if step == 0:
            products = gather_dots(state, slab, "dots_1")
    pieces, offsets = gather_rows(state)
    squares = call(squares_kernel, shape((8, PAD)), pieces, name="squares")
    squares = jnp.stack([squares] + [exchange("px", squares, k) for k in (2, 3, 1)])
    return call(
        functools.partial(finish_kernel, offsets),
        shape((8, slab_pixels)),
        (*pieces, squares),
        name="finish",
    )


def solution(mesh):
    in_specs = (
        P(None, "rows"),
        P("rows"),
        P("rows", "px"),
        P("px"),
        P(),
        P("rows", "px"),
        P("rows"),
        P(),
    )
    out_specs = P(None, "px")
    return jax.shard_map(shards, mesh=mesh, in_specs=in_specs, out_specs=out_specs, check_vma=False)
```
